512 devices in a mesh: wide: 64 (over y, z_lo, x), narrow: 8 (over z_hi, core).
Axes of the slice: x: 4, y: 4, z: 16 (z_hi: 4, z_lo: 4; z = z_hi * 4 + z_lo), core: 2. Of those that a mesh axis runs over, the one named last changes fastest.
Arguments:
- inputs: bfloat16 [512, 6144], P('wide', 'narrow'), may hold values from -6 to 6
- upstream_output_gradient: bfloat16 [512, 6144], P('wide', 'narrow'), may hold values from -6 to 6
- input_weight_frozen: bfloat16 [6144, 24576], P('narrow', 'wide'), may hold values from -0.078125 to 0.078125
- output_weight_frozen: bfloat16 [24576, 6144], P('wide', 'narrow'), may hold values from -0.0390625 to 0.0390625
- input_down_factor: bfloat16 [64, 6144], P(None, 'narrow'), may hold values from -0.078125 to 0.078125
- input_up_factor: bfloat16 [64, 24576], P(None, 'wide'), may hold values from -0.0390625 to 0.0390625
- output_down_factor: bfloat16 [64, 24576], P(None, 'wide'), may hold values from -0.0390625 to 0.0390625
- up_out: bfloat16 [64, 6144], P(None, 'narrow'), may hold values from -0.078125 to 0.078125
Outputs:
- gradient_input_rows: bfloat16 [512, 6144], P('wide', 'narrow')
- input_down_gradient: float32 [64, 6144], P(None, 'narrow')
- input_up_gradient: float32 [64, 24576], P(None, 'wide')
- output_down_gradient: float32 [64, 24576], P(None, 'wide')
- output_up_gradient: float32 [64, 6144], P(None, 'narrow')
The draws below stay inside these ranges and needn't reach their ends.
All inputs are finite; a program needn't handle non-finite values.
Results may differ from the reference program's by a relative error of at most 0.0051.
Values may be sent and summed in bfloat16 or wider, within the bound.
A program may use at most 64 MiB of HBM per device.

```python
import math
import jax
import jax.numpy as jnp

D = 6144
FF = 24576
R = 64
TOKENS = 512


def level_of(key, shape, cuts, low, high):
    def one(position, blocks):
        heights = jax.random.uniform(jax.random.fold_in(jax.random.fold_in(key, 6), position), (blocks,), jnp.float32, low / len(cuts), high / len(cuts))
        return jnp.repeat(jnp.exp(heights), shape[position] // blocks).reshape((-1,) + (1,) * (len(shape) - position - 1))

    level = one(*cuts[0])
    for cut in cuts[1:]:
        level = level * one(*cut)
    return level


def normal_values(own_key, extent, scale, reach, shards=(), dtype=jnp.bfloat16):
    factor_of = level_of(own_key, extent, shards, -0.22, 0.18) if shards else 1.0
    drawn = jax.random.normal(own_key, extent, jnp.float32) * scale * factor_of
    return jnp.minimum(jnp.maximum(drawn, -reach), reach).astype(dtype)


def setup_inputs(seed: int = 0) -> dict:
    streams_of = jax.random.split(jax.random.key(seed), 9)
    return {
        "inputs": normal_values(streams_of[0], (TOKENS, D), 1.0, 6.0, ((0, 64), (1, 8))),
        "upstream_output_gradient": normal_values(streams_of[1], (TOKENS, D), 1.0, 6.0, ((0, 64), (1, 8))),
        "input_weight_frozen": normal_values(streams_of[2], (D, FF), D ** -0.5, 0.078125, ((0, 8), (1, 64))),
        "output_weight_frozen": normal_values(streams_of[3], (FF, D), FF ** -0.5, 0.0390625, ((0, 64), (1, 8))),
        "input_down_factor": normal_values(streams_of[4], (R, D), D ** -0.5, 0.078125, ((1, 8),)),
        "input_up_factor": normal_values(streams_of[5], (R, FF), FF ** -0.5, 0.0390625, ((1, 64),)),
        "output_down_factor": normal_values(streams_of[6], (R, FF), FF ** -0.5, 0.0390625, ((1, 64),)),
        "up_out": normal_values(streams_of[7], (R, D), D ** -0.5, 0.078125, ((1, 8),)),
    }


adapter_scaling = 2.0
gelu_coef = math.sqrt(2.0 / math.pi)

def gelu_value(value):
    inner = jnp.tanh(gelu_coef * (value + 0.044715 * value * value * value))
    return 0.5 * value * (1.0 + inner)

def gelu_slope(value):
    inner = jnp.tanh(gelu_coef * (value + 0.044715 * value * value * value))
    return 0.5 * (1.0 + inner) + 0.5 * value * (1.0 - inner * inner) * gelu_coef * (1.0 + 3.0 * 0.044715 * value * value)

def reference(inputs, upstream_output_gradient, input_weight_frozen, output_weight_frozen, input_down_factor, input_up_factor, output_down_factor, up_out):
    input_rank_product = jnp.dot(inputs, input_down_factor.T, preferred_element_type=jnp.float32).astype(jnp.bfloat16)
    hidden_preactivation = jnp.dot(inputs, input_weight_frozen, preferred_element_type=jnp.float32) + adapter_scaling * jnp.dot(input_rank_product, input_up_factor, preferred_element_type=jnp.float32)
    activated_hidden = gelu_value(hidden_preactivation).astype(jnp.bfloat16)
    gradient_rank_product = jnp.dot(upstream_output_gradient, up_out.T, preferred_element_type=jnp.float32).astype(jnp.bfloat16)
    activated_gradient = jnp.dot(upstream_output_gradient, output_weight_frozen.T, preferred_element_type=jnp.float32) + adapter_scaling * jnp.dot(gradient_rank_product, output_down_factor, preferred_element_type=jnp.float32)
    preactivation_gradient = (activated_gradient * gelu_slope(hidden_preactivation)).astype(jnp.bfloat16)
    activation_rank_product = jnp.dot(activated_hidden, output_down_factor.T, preferred_element_type=jnp.float32).astype(jnp.bfloat16)
    backward_rank_product = jnp.dot(preactivation_gradient, input_up_factor.T, preferred_element_type=jnp.float32).astype(jnp.bfloat16)
    input_down_gradient = adapter_scaling * jnp.dot(backward_rank_product.T, inputs, preferred_element_type=jnp.float32)
    input_up_gradient = adapter_scaling * jnp.dot(input_rank_product.T, preactivation_gradient, preferred_element_type=jnp.float32)
    output_down_gradient = adapter_scaling * jnp.dot(gradient_rank_product.T, activated_hidden, preferred_element_type=jnp.float32)
    output_up_gradient = adapter_scaling * jnp.dot(activation_rank_product.T, upstream_output_gradient, preferred_element_type=jnp.float32)
    gradient_input_rows = jnp.dot(preactivation_gradient, input_weight_frozen.T, preferred_element_type=jnp.float32) + adapter_scaling * jnp.dot(backward_rank_product, input_down_factor, preferred_element_type=jnp.float32)
    return (gradient_input_rows.astype(jnp.bfloat16), input_down_gradient, input_up_gradient, output_down_gradient, output_up_gradient)
```

```python
import functools
import math

import jax
import jax.numpy as jnp
from jax import lax
from jax.experimental import pallas as pl
from jax.experimental.pallas import tpu as pltpu
from jax.sharding import PartitionSpec as P

MESH = pl.DeviceIdType.MESH
F32 = jnp.float32
BF16 = jnp.bfloat16
scaling = 2.0
coef = math.sqrt(2.0 / math.pi)

FAMILIES = (
    "gz", "ga", "gb", "gc", "gd", "core", "rz", "pz", "pc", "fx", "fy", "fz", "nz", "nc",
    "ec", "ez", "eg", "eh", "ya", "xa", "xb", "yb", "cz", "spare",
)
FAMILY = {name: i for i, name in enumerate(FAMILIES)}


def nn(left, right):
    return lax.dot_general(left, right, (((1,), (0,)), ((), ())), preferred_element_type=F32)


def nt(left, right):
    return lax.dot_general(left, right, (((1,), (1,)), ((), ())), preferred_element_type=F32)


def tn(left, right):
    return lax.dot_general(left, right, (((0,), (0,)), ((), ())), preferred_element_type=F32)


def kernel(
    x_ref, g_ref, w1_hbm, w2_hbm, din_ref, upin_ref, dout_ref, upout_ref,
    dx_ref, gdin_ref, gupin_ref, gdout_ref, gupout_ref,
    w1, w2, zbuf, strip, part_out, part_in, part_own, red_out, red_in,
    pre, proj, fxb, fyb, fzb, eown, ein, ezout, ezin, egb,
    dxp, c1in, c2out, c2in, czout, czin,
    wsem, ssem, rsem,
):
    w = lax.axis_index("wide")
    n = lax.axis_index("narrow")
    y, z, x = w // 16, (w // 4) % 4, w % 4
    zh, c = n // 2, n % 2
    oc = 1 - c

    def at_x(d):
        return (y * 16 + z * 4 + (x + d) % 4, n)

    def at_y(d):
        return (((y + d) % 4) * 16 + z * 4 + x, n)

    def at_z(d):
        return (y * 16 + ((z + d) % 4) * 4 + x, n)

    def at_h(d):
        return (w, ((zh + d) % 4) * 2 + c)

    other = (w, zh * 2 + oc)
    sent = []

    def push(family, slot, src, dst, to):
        i = FAMILY[family]
        copy = pltpu.make_async_remote_copy(
            src_ref=src, dst_ref=dst, send_sem=ssem.at[i, slot], recv_sem=rsem.at[i, slot],
            device_id=to, device_id_type=MESH,
        )
        copy.start()
        sent.append(copy)
        return copy

    load1 = pltpu.make_async_copy(w1_hbm, w1, wsem.at[0])
    load2 = pltpu.make_async_copy(w2_hbm, w2, wsem.at[1])
    load1.start()
    load2.start()

    barrier = pltpu.get_barrier_semaphore()
    for d in (1, 2, 3):
        for at in (at_x, at_y, at_z, at_h):
            pl.semaphore_signal(barrier, inc=1, device_id=at(d), device_id_type=MESH)
    pl.semaphore_signal(barrier, inc=1, device_id=other, device_id_type=MESH)

    zbuf[z] = jnp.concatenate([x_ref[...].astype(F32), g_ref[...].astype(F32)], 0).astype(BF16)
    pl.semaphore_wait(barrier, 13)

    copies = [push("gz", d, zbuf.at[z], zbuf.at[z], at_z(d)) for d in (2, 1, 3)]
    for copy in copies:
        copy.wait_recv()
    planes = [zbuf[i].astype(F32) for i in range(4)]
    for t in range(2):
        rows = slice(8 * t, 8 * t + 8)
        strip[0, y, t, x] = jnp.concatenate([planes[0][rows], planes[1][rows]], 0).astype(BF16)
        strip[1, x, t, y] = jnp.concatenate([planes[2][rows], planes[3][rows]], 0).astype(BF16)
    copies = []
    for d in (2, 1, 3):
        mine = strip.at[0, y, :, x]
        copies.append(push("ga", d, mine, mine, at_x(d)))
        mine = strip.at[1, x, :, y]
        copies.append(push("gb", d, mine, mine, at_y(d)))
    for copy in copies:
        copy.wait_recv()
    copies = []
    for d in (2, 1, 3):
        mine = strip.at[0, y]
        copies.append(push("gc", d, mine, mine, at_y(d)))
        mine = strip.at[1, x]
        copies.append(push("gd", d, mine, mine, at_x(d)))
    load1.wait()
    load2.wait()
    for copy in copies:
        copy.wait_recv()

    def partial(half, store):
        xs = strip[half, :, 0].reshape(256, 768)
        gs = strip[half, :, 1].reshape(256, 768)
        store(0, 384, nn(xs, w1[...]))
        store(384, 384, nt(gs, w2[...]))
        store(768, 64, nt(xs, din_ref[...]))
        store(832, 64, nt(gs, upout_ref[...]))

    def store_out(start, size, value):
        part_out[:, :, start:start + size] = value.astype(BF16).reshape(4, 64, size)

    def store_own(start, size, value):
        part_own[:, :, start:start + size] = value.reshape(4, 64, size)

    partial(oc, store_out)
    copy = push("core", 0, part_out, part_in, other)
    partial(c, store_own)
    copy.wait_recv()
    copies = []
    for d in (2, 1, 3):
        k = (zh + d) % 4
        red_out[d] = (part_own[k] + part_in[k].astype(F32)).astype(BF16)
        copies.append(push("rz", d, red_out.at[d], red_in.at[d], at_h(d)))
    total = part_own[zh] + part_in[zh].astype(F32)
    for copy in copies:
        copy.wait_recv()
    for d in (1, 2, 3):
        total = total + red_in[d].astype(F32)

    proj_in = total[:, 768:832].astype(BF16)
    proj_grad = total[:, 832:896].astype(BF16)
    v = total[:, :384] + scaling * nn(proj_in, upin_ref[...])
    grad = total[:, 384:768] + scaling * nn(proj_grad, dout_ref[...])
    t = jnp.tanh(coef * (v + 0.044715 * v * v * v))
    act = (0.5 * v * (1.0 + t)).astype(BF16)
    slope = 0.5 * (1.0 + t) + 0.5 * v * (1.0 - t * t) * coef * (1.0 + 3.0 * 0.044715 * v * v)
    pre_own = (grad * slope).astype(BF16)

    pre[c, zh] = pre_own
    mine = pre.at[c, zh]
    pz = {d: push("pz", d, mine, mine, at_h(d)) for d in (2, 1, 3)}
    pc = [push("pc", 0, mine, mine, other)]

    fxb[x] = jnp.concatenate([nt(act, dout_ref[...]), nt(pre_own, upin_ref[...])], 1)
    fx = [push("fx", d, fxb.at[x], fxb.at[x], at_x(d)) for d in (2, 1, 3)]
    eown[0] = scaling * tn(proj_in, pre_own)
    eown[1] = scaling * tn(proj_grad, act)
    ec = push("ec", 0, eown.at[oc], ein, other)

    for copy in fx:
        copy.wait_recv()
    fyb[y] = fxb[0] + fxb[1] + fxb[2] + fxb[3]
    fy = [push("fy", d, fyb.at[y], fyb.at[y], at_y(d)) for d in (2, 1, 3)]

    ec.wait_recv()
    esum = eown[c] + ein[...]
    ezout[...] = esum.astype(BF16).reshape(4, 16, 384)
    ez = [push("ez", d, ezout.at[(zh + d) % 4], ezin.at[d], at_h(d)) for d in (2, 1, 3)]

    for copy in fy:
        copy.wait_recv()
    fzb[z] = fyb[0] + fyb[1] + fyb[2] + fyb[3]
    fz = [push("fz", d, fzb.at[z], fzb.at[z], at_z(d)) for d in (2, 1, 3)]

    for d in (1, 3, 2):
        pz[d].wait_recv()
        got = pre.at[c, (zh + 4 - d) % 4]
        pc.append(push("pc", d, got, got, other))

    for copy in fz:
        copy.wait_recv()
    proj[c, zh] = (fzb[0] + fzb[1] + fzb[2] + fzb[3]).astype(BF16)
    mine = proj.at[c, zh]
    nz = {d: push("nz", d, mine, mine, at_h(d)) for d in (2, 1, 3)}
    nc = [push("nc", 0, mine, mine, other)]

    for copy in pc:
        copy.wait_recv()
    for h in range(2):
        rows = pre[h].reshape(256, 384)
        dxp[h] = nt(rows, w1[...]).astype(BF16).reshape(4, 4, 16, 768)
    c1 = []
    for d in (2, 1, 3):
        c1.append(push("ya", d, dxp.at[0, (y + d) % 4], c1in.at[0, d], at_y(d)))
        c1.append(push("xb", d, dxp.at[1, (x + d) % 4], c1in.at[1, d], at_x(d)))

    for copy in ez:
        copy.wait_recv()
    esl = ezout[zh].astype(F32)
    for d in (1, 2, 3):
        esl = esl + ezin[d].astype(F32)
    egb[c, zh] = esl.astype(BF16)
    mine = egb.at[c, zh]
    eg = {d: push("eg", d, mine, mine, at_h(d)) for d in (2, 1, 3)}
    eh = [push("eh", 0, mine, mine, other)]

    for copy in c1:
        copy.wait_recv()
    c2 = []
    s0 = dxp[0, y].astype(F32)
    s1 = dxp[1, x].astype(F32)
    for d in (1, 2, 3):
        s0 = s0 + c1in[0, d].astype(F32)
        s1 = s1 + c1in[1, d].astype(F32)
    c2out[0] = s0.astype(BF16)
    c2out[1] = s1.astype(BF16)
    for d in (2, 1, 3):
        c2.append(push("xa", d, c2out.at[0, (x + d) % 4], c2in.at[0, d], at_x(d)))
        c2.append(push("yb", d, c2out.at[1, (y + d) % 4], c2in.at[1, d], at_y(d)))

    for d in (1, 3, 2):
        nz[d].wait_recv()
        got = proj.at[c, (zh + 4 - d) % 4]
        nc.append(push("nc", d, got, got, other))

    for copy in c2:
        copy.wait_recv()
    s0 = c2out[0, x].astype(F32)
    s1 = c2out[1, y].astype(F32)
    for d in (1, 2, 3):
        s0 = s0 + c2in[0, d].astype(F32)
        s1 = s1 + c2in[1, d].astype(F32)
    czout[0] = s0[:8]
    czout[1] = s0[8:]
    czout[2] = s1[:8]
    czout[3] = s1[8:]
    cz = [push("cz", d, czout.at[(z + d) % 4], czin.at[d], at_z(d)) for d in (2, 1, 3)]

    for d in (1, 3, 2):
        eg[d].wait_recv()
        got = egb.at[c, (zh + 4 - d) % 4]
        eh.append(push("eh", d, got, got, other))

    for copy in nc:
        copy.wait_recv()
    rank = proj[...].reshape(512, 128)
    xs = strip[:, :, 0].reshape(512, 768)
    gs = strip[:, :, 1].reshape(512, 768)
    gupout_ref[...] = scaling * tn(rank[:, :64], gs)
    gdin_ref[...] = scaling * tn(rank[:, 64:], xs)

    for copy in eh:
        copy.wait_recv()
    gupin_ref[...] = egb[0].reshape(64, 384).astype(F32)
    gdout_ref[...] = egb[1].reshape(64, 384).astype(F32)

    half = z // 2
    k = jnp.where(half == 0, y, x)
    j = jnp.where(half == 0, x, y)
    rows = proj[half, k, pl.ds(pl.multiple_of(j * 16, 16), 16), :].astype(F32)
    back = jnp.where(z % 2 == 0, rows[:8], rows[8:])[:, 64:].astype(BF16)
    extra = scaling * nn(back, din_ref[...])
    for copy in cz:
        copy.wait_recv()
    out = czout[z] + extra
    for d in (1, 2, 3):
        out = out + czin[d]
    dx_ref[...] = out.astype(BF16)

    for copy in sent:
        copy.wait_send()


def shards(x, g, w1, w2, din, upin, dout, upout):
    vmem = pl.BlockSpec(memory_space=pltpu.VMEM)
    hbm = pl.BlockSpec(memory_space=pl.ANY)
    nf = len(FAMILIES)
    return pl.pallas_call(
        kernel,
        out_shape=(
            jax.ShapeDtypeStruct((8, 768), BF16),
            jax.ShapeDtypeStruct((64, 768), F32),
            jax.ShapeDtypeStruct((64, 384), F32),
            jax.ShapeDtypeStruct((64, 384), F32),
            jax.ShapeDtypeStruct((64, 768), F32),
        ),
        in_specs=[vmem, vmem, hbm, hbm, vmem, vmem, vmem, vmem],
        out_specs=(vmem,) * 5,
        scratch_shapes=[
            pltpu.VMEM((768, 384), BF16),
            pltpu.VMEM((384, 768), BF16),
            pltpu.VMEM((4, 16, 768), BF16),
            pltpu.VMEM((2, 4, 2, 4, 16, 768), BF16),
            pltpu.VMEM((4, 64, 896), BF16),
            pltpu.VMEM((4, 64, 896), BF16),
            pltpu.VMEM((4, 64, 896), F32),
            pltpu.VMEM((4, 64, 896), BF16),
            pltpu.VMEM((4, 64, 896), BF16),
            pltpu.VMEM((2, 4, 64, 384), BF16),
            pltpu.VMEM((2, 4, 64, 128), BF16),
            pltpu.VMEM((4, 64, 128), F32),
            pltpu.VMEM((4, 64, 128), F32),
            pltpu.VMEM((4, 64, 128), F32),
            pltpu.VMEM((2, 64, 384), F32),
            pltpu.VMEM((64, 384), F32),
            pltpu.VMEM((4, 16, 384), BF16),
            pltpu.VMEM((4, 16, 384), BF16),
            pltpu.VMEM((2, 4, 16, 384), BF16),
            pltpu.VMEM((2, 4, 4, 16, 768), BF16),
            pltpu.VMEM((2, 4, 4, 16, 768), BF16),
            pltpu.VMEM((2, 4, 16, 768), BF16),
            pltpu.VMEM((2, 4, 16, 768), BF16),
            pltpu.VMEM((4, 8, 768), F32),
            pltpu.VMEM((4, 8, 768), F32),
            pltpu.SemaphoreType.DMA((2,)),
            pltpu.SemaphoreType.DMA((nf, 4)),
            pltpu.SemaphoreType.DMA((nf, 4)),
        ],
        compiler_params=pltpu.CompilerParams(
            collective_id=0, has_side_effects=True, vmem_limit_bytes=48 * 1024 * 1024
        ),
    )(x, g, w1, w2, din, upin, dout, upout)


def solution(mesh):
    return jax.shard_map(
        shards,
        mesh=mesh,
        in_specs=(
            P("wide", "narrow"),
            P("wide", "narrow"),
            P("narrow", "wide"),
            P("wide", "narrow"),
            P(None, "narrow"),
            P(None, "wide"),
            P(None, "wide"),
            P(None, "narrow"),
        ),
        out_specs=(
            P("wide", "narrow"),
            P(None, "narrow"),
            P(None, "wide"),
            P(None, "wide"),
            P(None, "narrow"),
        ),
        check_vma=False,
    )
```

```python
import functools
import math

import jax
import jax.numpy as jnp
from jax import lax
from jax.experimental import pallas as pl
from jax.experimental.pallas import tpu as pltpu
from jax.sharding import PartitionSpec as P

MESH = pl.DeviceIdType.MESH
F32 = jnp.float32
BF16 = jnp.bfloat16
scaling = 2.0
coef = math.sqrt(2.0 / math.pi)

FAMILIES = (
    "gz", "ga", "gb", "gc", "gd", "core", "rz", "pz", "pc", "fx", "fy", "fz", "nz", "nc",
    "ec", "ez", "eg", "eh", "ya", "xa", "xb", "yb", "cz", "spare",
)
FAMILY = {name: i for i, name in enumerate(FAMILIES)}


def nn(left, right):
    return lax.dot_general(left, right, (((1,), (0,)), ((), ())), preferred_element_type=F32)


def nt(left, right):
    return lax.dot_general(left, right, (((1,), (1,)), ((), ())), preferred_element_type=F32)


def tn(left, right):
    return lax.dot_general(left, right, (((0,), (0,)), ((), ())), preferred_element_type=F32)


def kernel(
    x_hbm, g_hbm, w1_hbm, w2_hbm, din_hbm, upin_hbm, dout_hbm, upout_hbm,
    dx_ref, gdin_ref, gupin_ref, gdout_ref, gupout_ref,
    x_ref, g_ref, w1, w2, din_ref, upin_ref, dout_ref, upout_ref, zbuf, strip, part_out, part_in, part_own, red_out, red_in,
    pre, proj, fxb, fyb, fzb, eown, ein, ezout, ezin, egb,
    dxp, c1in, c2out, c2in, czout, czin,
    wsem, ssem, rsem,
):
    w = lax.axis_index("wide")
    n = lax.axis_index("narrow")
    y, z, x = w // 16, (w // 4) % 4, w % 4
    zh, c = n // 2, n % 2
    oc = 1 - c

    def at_x(d):
        return (y * 16 + z * 4 + (x + d) % 4, n)

    def at_y(d):
        return (((y + d) % 4) * 16 + z * 4 + x, n)

    def at_z(d):
        return (y * 16 + ((z + d) % 4) * 4 + x, n)

    def at_h(d):
        return (w, ((zh + d) % 4) * 2 + c)

    other = (w, zh * 2 + oc)
    sent = []

    def push(family, slot, src, dst, to):
        i = FAMILY[family]
        copy = pltpu.make_async_remote_copy(
            src_ref=src, dst_ref=dst, send_sem=ssem.at[i, slot], recv_sem=rsem.at[i, slot],
            device_id=to, device_id_type=MESH,
        )
        copy.start()
        sent.append(copy)
        return copy

    loads = [
        pltpu.make_async_copy(src, dst, wsem.at[i])
        for i, (src, dst) in enumerate((
            (x_hbm, x_ref), (g_hbm, g_ref), (w1_hbm, w1), (w2_hbm, w2), (din_hbm, din_ref),
            (upin_hbm, upin_ref), (dout_hbm, dout_ref), (upout_hbm, upout_ref),
        ))
    ]
    for load in loads:
        load.start()

    barrier = pltpu.get_barrier_semaphore()
    for d in (1, 2, 3):
        for at in (at_x, at_y, at_z, at_h):
            pl.semaphore_signal(barrier, inc=1, device_id=at(d), device_id_type=MESH)
    pl.semaphore_signal(barrier, inc=1, device_id=other, device_id_type=MESH)

    loads[0].wait()
    loads[1].wait()
    zbuf[z] = jnp.concatenate([x_ref[...].astype(F32), g_ref[...].astype(F32)], 0).astype(BF16)
    pl.semaphore_wait(barrier, 13)

    copies = [push("gz", d, zbuf.at[z], zbuf.at[z], at_z(d)) for d in (2, 1, 3)]
    for copy in copies:
        copy.wait_recv()
    planes = [zbuf[i].astype(F32) for i in range(4)]
    for t in range(2):
        rows = slice(8 * t, 8 * t + 8)
        strip[0, y, t, x] = jnp.concatenate([planes[0][rows], planes[1][rows]], 0).astype(BF16)
        strip[1, x, t, y] = jnp.concatenate([planes[2][rows], planes[3][rows]], 0).astype(BF16)
    copies = []
    for d in (2, 1, 3):
        mine = strip.at[0, y, :, x]
        copies.append(push("ga", d, mine, mine, at_x(d)))
        mine = strip.at[1, x, :, y]
        copies.append(push("gb", d, mine, mine, at_y(d)))
    for copy in copies:
        copy.wait_recv()
    copies = []
    for d in (2, 1, 3):
        mine = strip.at[0, y]
        copies.append(push("gc", d, mine, mine, at_y(d)))
        mine = strip.at[1, x]
        copies.append(push("gd", d, mine, mine, at_x(d)))
    for load in loads[2:]:
        load.wait()
    for copy in copies:
        copy.wait_recv()

    def partial(half, store):
        xs = strip[half, :, 0].reshape(256, 768)
        gs = strip[half, :, 1].reshape(256, 768)
        store(0, 384, nn(xs, w1[...]))
        store(384, 384, nt(gs, w2[...]))
        store(768, 64, nt(xs, din_ref[...]))
        store(832, 64, nt(gs, upout_ref[...]))

    def store_out(start, size, value):
        part_out[:, :, start:start + size] = value.reshape(4, 64, size)

    def store_own(start, size, value):
        part_own[:, :, start:start + size] = value.reshape(4, 64, size)

    partial(oc, store_out)
    copy = push("core", 0, part_out, part_in, other)
    partial(c, store_own)
    copy.wait_recv()
    copies = []
    for d in (2, 1, 3):
        k = (zh + d) % 4
        red_out[d] = (part_own[k] + part_in[k]).astype(BF16)
        copies.append(push("rz", d, red_out.at[d], red_in.at[d], at_h(d)))
    total = part_own[zh] + part_in[zh]
    for copy in copies:
        copy.wait_recv()
    for d in (1, 2, 3):
        total = total + red_in[d].astype(F32)

    proj_in = total[:, 768:832].astype(BF16)
    proj_grad = total[:, 832:896].astype(BF16)
    v = total[:, :384] + scaling * nn(proj_in, upin_ref[...])
    grad = total[:, 384:768] + scaling * nn(proj_grad, dout_ref[...])
    t = jnp.tanh(coef * (v + 0.044715 * v * v * v))
    act = (0.5 * v * (1.0 + t)).astype(BF16)
    slope = 0.5 * (1.0 + t) + 0.5 * v * (1.0 - t * t) * coef * (1.0 + 3.0 * 0.044715 * v * v)
    pre_own = (grad * slope).astype(BF16)

    pre[c, zh] = pre_own
    mine = pre.at[c, zh]
    pz = {d: push("pz", d, mine, mine, at_h(d)) for d in (2, 1, 3)}
    pc = [push("pc", 0, mine, mine, other)]

    fxb[x] = jnp.concatenate([nt(act, dout_ref[...]), nt(pre_own, upin_ref[...])], 1)
    fx = [push("fx", d, fxb.at[x], fxb.at[x], at_x(d)) for d in (2, 1, 3)]
    eown[0] = scaling * tn(proj_in, pre_own)
    eown[1] = scaling * tn(proj_grad, act)
    ec = push("ec", 0, eown.at[oc], ein, other)

    for copy in fx:
        copy.wait_recv()
    fyb[y] = fxb[0] + fxb[1] + fxb[2] + fxb[3]
    fy = [push("fy", d, fyb.at[y], fyb.at[y], at_y(d)) for d in (2, 1, 3)]

    ec.wait_recv()
    esum = eown[c] + ein[...]
    ezout[...] = esum.astype(BF16).reshape(4, 16, 384)
    ez = [push("ez", d, ezout.at[(zh + d) % 4], ezin.at[d], at_h(d)) for d in (2, 1, 3)]

    for copy in fy:
        copy.wait_recv()
    fzb[z] = fyb[0] + fyb[1] + fyb[2] + fyb[3]
    fz = [push("fz", d, fzb.at[z], fzb.at[z], at_z(d)) for d in (2, 1, 3)]

    for d in (1, 3, 2):
        pz[d].wait_recv()
        got = pre.at[c, (zh + 4 - d) % 4]
        pc.append(push("pc", d, got, got, other))

    for copy in fz:
        copy.wait_recv()
    proj[c, zh] = (fzb[0] + fzb[1] + fzb[2] + fzb[3]).astype(BF16)
    mine = proj.at[c, zh]
    nz = {d: push("nz", d, mine, mine, at_h(d)) for d in (2, 1, 3)}
    nc = [push("nc", 0, mine, mine, other)]

    for copy in pc:
        copy.wait_recv()
    for h in range(2):
        rows = pre[h].reshape(256, 384)
        dxp[h] = nt(rows, w1[...]).astype(BF16).reshape(4, 4, 16, 768)
    c1 = []
    for d in (2, 1, 3):
        c1.append(push("ya", d, dxp.at[0, (y + d) % 4], c1in.at[0, d], at_y(d)))
        c1.append(push("xb", d, dxp.at[1, (x + d) % 4], c1in.at[1, d], at_x(d)))

    for copy in ez:
        copy.wait_recv()
    esl = ezout[zh].astype(F32)
    for d in (1, 2, 3):
        esl = esl + ezin[d].astype(F32)
    egb[c, zh] = esl.astype(BF16)
    mine = egb.at[c, zh]
    eg = {d: push("eg", d, mine, mine, at_h(d)) for d in (2, 1, 3)}
    eh = [push("eh", 0, mine, mine, other)]

    for copy in c1:
        copy.wait_recv()
    c2 = []
    s0 = dxp[0, y].astype(F32)
    s1 = dxp[1, x].astype(F32)
    for d in (1, 2, 3):
        s0 = s0 + c1in[0, d].astype(F32)
        s1 = s1 + c1in[1, d].astype(F32)
    c2out[0] = s0
    c2out[1] = s1
    for d in (2, 1, 3):
        c2.append(push("xa", d, c2out.at[0, (x + d) % 4], c2in.at[0, d], at_x(d)))
        c2.append(push("yb", d, c2out.at[1, (y + d) % 4], c2in.at[1, d], at_y(d)))

    for d in (1, 3, 2):
        nz[d].wait_recv()
        got = proj.at[c, (zh + 4 - d) % 4]
        nc.append(push("nc", d, got, got, other))

    for copy in c2:
        copy.wait_recv()
    s0 = c2out[0, x]
    s1 = c2out[1, y]
    for d in (1, 2, 3):
        s0 = s0 + c2in[0, d]
        s1 = s1 + c2in[1, d]
    czout[0] = s0[:8]
    czout[1] = s0[8:]
    czout[2] = s1[:8]
    czout[3] = s1[8:]
    cz = [push("cz", d, czout.at[(z + d) % 4], czin.at[d], at_z(d)) for d in (2, 1, 3)]

    for d in (1, 3, 2):
        eg[d].wait_recv()
        got = egb.at[c, (zh + 4 - d) % 4]
        eh.append(push("eh", d, got, got, other))

    for copy in nc:
        copy.wait_recv()
    rank = proj[...].reshape(512, 128)
    xs = strip[:, :, 0].reshape(512, 768)
    gs = strip[:, :, 1].reshape(512, 768)
    gupout_ref[...] = scaling * tn(rank[:, :64], gs)
    gdin_ref[...] = scaling * tn(rank[:, 64:], xs)

    for copy in eh:
        copy.wait_recv()
    gupin_ref[...] = egb[0].reshape(64, 384).astype(F32)
    gdout_ref[...] = egb[1].reshape(64, 384).astype(F32)

    half = z // 2
    k = jnp.where(half == 0, y, x)
    j = jnp.where(half == 0, x, y)
    rows = proj[half, k, pl.ds(pl.multiple_of(j * 16, 16), 16), :].astype(F32)
    back = jnp.where(z % 2 == 0, rows[:8], rows[8:])[:, 64:].astype(BF16)
    extra = scaling * nn(back, din_ref[...])
    for copy in cz:
        copy.wait_recv()
    out = czout[z] + extra
    for d in (1, 2, 3):
        out = out + czin[d]
    dx_ref[...] = out.astype(BF16)

    for copy in sent:
        copy.wait_send()


def hand_over(*refs):
    sems = refs[10]
    copies = [pltpu.make_async_copy(refs[i], refs[5 + i], sems.at[i]) for i in range(5)]
    for copy in copies:
        copy.start()
    for copy in copies:
        copy.wait()


def shards(x, g, w1, w2, din, upin, dout, upout):
    vmem = pl.BlockSpec(memory_space=pltpu.VMEM)
    hbm = pl.BlockSpec(memory_space=pl.ANY)
    nf = len(FAMILIES)
    shapes = (
        jax.ShapeDtypeStruct((8, 768), BF16),
        jax.ShapeDtypeStruct((64, 768), F32),
        jax.ShapeDtypeStruct((64, 384), F32),
        jax.ShapeDtypeStruct((64, 384), F32),
        jax.ShapeDtypeStruct((64, 768), F32),
    )
    made = pl.pallas_call(
        kernel,
        out_shape=shapes,
        in_specs=[hbm] * 8,
        out_specs=(vmem,) * 5,
        scratch_shapes=[
            pltpu.VMEM((8, 768), BF16),
            pltpu.VMEM((8, 768), BF16),
            pltpu.VMEM((768, 384), BF16),
            pltpu.VMEM((384, 768), BF16),
            pltpu.VMEM((64, 768), BF16),
            pltpu.VMEM((64, 384), BF16),
            pltpu.VMEM((64, 384), BF16),
            pltpu.VMEM((64, 768), BF16),
            pltpu.VMEM((4, 16, 768), BF16),
            pltpu.VMEM((2, 4, 2, 4, 16, 768), BF16),
            pltpu.VMEM((4, 64, 896), F32),
            pltpu.VMEM((4, 64, 896), F32),
            pltpu.VMEM((4, 64, 896), F32),
            pltpu.VMEM((4, 64, 896), BF16),
            pltpu.VMEM((4, 64, 896), BF16),
            pltpu.VMEM((2, 4, 64, 384), BF16),
            pltpu.VMEM((2, 4, 64, 128), BF16),
            pltpu.VMEM((4, 64, 128), F32),
            pltpu.VMEM((4, 64, 128), F32),
            pltpu.VMEM((4, 64, 128), F32),
            pltpu.VMEM((2, 64, 384), F32),
            pltpu.VMEM((64, 384), F32),
            pltpu.VMEM((4, 16, 384), BF16),
            pltpu.VMEM((4, 16, 384), BF16),
            pltpu.VMEM((2, 4, 16, 384), BF16),
            pltpu.VMEM((2, 4, 4, 16, 768), BF16),
            pltpu.VMEM((2, 4, 4, 16, 768), BF16),
            pltpu.VMEM((2, 4, 16, 768), F32),
            pltpu.VMEM((2, 4, 16, 768), F32),
            pltpu.VMEM((4, 8, 768), F32),
            pltpu.VMEM((4, 8, 768), F32),
            pltpu.SemaphoreType.DMA((8,)),
            pltpu.SemaphoreType.DMA((nf, 4)),
            pltpu.SemaphoreType.DMA((nf, 4)),
        ],
        compiler_params=pltpu.CompilerParams(
            collective_id=0, has_side_effects=True, vmem_limit_bytes=60 * 1024 * 1024
        ),
    )(x, g, w1, w2, din, upin, dout, upout)
    return pl.pallas_call(
        hand_over,
        out_shape=shapes,
        in_specs=[hbm] * 5,
        out_specs=(hbm,) * 5,
        scratch_shapes=[pltpu.SemaphoreType.DMA((5,))],
        compiler_params=pltpu.CompilerParams(vmem_limit_bytes=60 * 1024 * 1024),
    )(*made)


def solution(mesh):
    return jax.shard_map(
        shards,
        mesh=mesh,
        in_specs=(
            P("wide", "narrow"),
            P("wide", "narrow"),
            P("narrow", "wide"),
            P("wide", "narrow"),
            P(None, "narrow"),
            P(None, "wide"),
            P(None, "wide"),
            P(None, "narrow"),
        ),
        out_specs=(
            P("wide", "narrow"),
            P(None, "narrow"),
            P(None, "wide"),
            P(None, "wide"),
            P(None, "narrow"),
        ),
        check_vma=False,
    )
```

```python
import functools
import math

import jax
import jax.numpy as jnp
from jax import lax
from jax.experimental import pallas as pl
from jax.experimental.pallas import tpu as pltpu
from jax.sharding import PartitionSpec as P

MESH = pl.DeviceIdType.MESH
F32 = jnp.float32
BF16 = jnp.bfloat16
scaling = 2.0
coef = math.sqrt(2.0 / math.pi)

FAMILIES = (
    "gz", "ga", "gb", "gc", "gd", "core", "rz", "pz", "pc", "fx", "fy", "fz", "nz", "nc",
    "ec", "ez", "eg", "eh", "ya", "xa", "xb", "yb", "cz", "spare",
)
FAMILY = {name: i for i, name in enumerate(FAMILIES)}


def nn(left, right):
    return lax.dot_general(left, right, (((1,), (0,)), ((), ())), preferred_element_type=F32)


def nt(left, right):
    return lax.dot_general(left, right, (((1,), (1,)), ((), ())), preferred_element_type=F32)


def tn(left, right):
    return lax.dot_general(left, right, (((0,), (0,)), ((), ())), preferred_element_type=F32)


def kernel(
    x_hbm, g_hbm, w1_hbm, w2_hbm, din_hbm, upin_hbm, dout_hbm, upout_hbm,
    dx_ref, gdin_ref, gupin_ref, gdout_ref, gupout_ref,
    x_ref, g_ref, w1, w2, din_ref, upin_ref, dout_ref, upout_ref, zbuf, strip, part_out, part_in, part_own, red_out, red_in,
    pre, proj, fxb, fyb, fzb, eown, ein, ezout, ezin, egb,
    dxp, c1in, c2out, c2in, czout, czin,
    wsem, ssem, rsem,
):
    w = lax.axis_index("wide")
    n = lax.axis_index("narrow")
    y, z, x = w // 16, (w // 4) % 4, w % 4
    zh, c = n // 2, n % 2
    oc = 1 - c

    def at_x(d):
        return (y * 16 + z * 4 + (x + d) % 4, n)

    def at_y(d):
        return (((y + d) % 4) * 16 + z * 4 + x, n)

    def at_z(d):
        return (y * 16 + ((z + d) % 4) * 4 + x, n)

    def at_h(d):
        return (w, ((zh + d) % 4) * 2 + c)

    other = (w, zh * 2 + oc)
    sent = []

    def push(family, slot, src, dst, to):
        i = FAMILY[family]
        copy = pltpu.make_async_remote_copy(
            src_ref=src, dst_ref=dst, send_sem=ssem.at[i, slot], recv_sem=rsem.at[i, slot],
            device_id=to, device_id_type=MESH,
        )
        copy.start()
        sent.append(copy)
        return copy

    loads = [
        pltpu.make_async_copy(src, dst, wsem.at[i])
        for i, (src, dst) in enumerate((
            (x_hbm, x_ref), (g_hbm, g_ref), (w1_hbm, w1), (w2_hbm, w2), (din_hbm, din_ref),
            (upin_hbm, upin_ref), (dout_hbm, dout_ref), (upout_hbm, upout_ref),
        ))
    ]
    for load in loads:
        load.start()

    barrier = pltpu.get_barrier_semaphore()
    for d in (1, 2, 3):
        for at in (at_x, at_y, at_z, at_h):
            pl.semaphore_signal(barrier, inc=1, device_id=at(d), device_id_type=MESH)
    pl.semaphore_signal(barrier, inc=1, device_id=other, device_id_type=MESH)

    loads[0].wait()
    loads[1].wait()
    zbuf[z] = jnp.concatenate([x_ref[...].astype(F32), g_ref[...].astype(F32)], 0).astype(BF16)
    pl.semaphore_wait(barrier, 13)

    copies = [push("gz", d, zbuf.at[z], zbuf.at[z], at_z(d)) for d in (2, 1, 3)]
    for copy in copies:
        copy.wait_recv()
    planes = [zbuf[i].astype(F32) for i in range(4)]
    for t in range(2):
        rows = slice(8 * t, 8 * t + 8)
        strip[0, y, t, x] = jnp.concatenate([planes[0][rows], planes[1][rows]], 0).astype(BF16)
        strip[1, x, t, y] = jnp.concatenate([planes[2][rows], planes[3][rows]], 0).astype(BF16)
    copies = []
    for d in (2, 1, 3):
        mine = strip.at[0, y, :, x]
        copies.append(push("ga", d, mine, mine, at_x(d)))
        mine = strip.at[1, x, :, y]
        copies.append(push("gb", d, mine, mine, at_y(d)))
    for copy in copies:
        copy.wait_recv()
    copies = []
    for d in (2, 1, 3):
        mine = strip.at[0, y]
        copies.append(push("gc", d, mine, mine, at_y(d)))
        mine = strip.at[1, x]
        copies.append(push("gd", d, mine, mine, at_x(d)))
    for load in loads[2:]:
        load.wait()
    for copy in copies:
        copy.wait_recv()

    def partial(half, store):
        xs = strip[half, :, 0].reshape(256, 768)
        gs = strip[half, :, 1].reshape(256, 768)
        store(0, 384, nn(xs, w1[...]))
        store(384, 384, nt(gs, w2[...]))
        store(768, 64, nt(xs, din_ref[...]))
        store(832, 64, nt(gs, upout_ref[...]))

    def store_out(start, size, value):
        part_out[:, :, start:start + size] = value.reshape(4, 64, size)

    def store_own(start, size, value):
        part_own[:, :, start:start + size] = value.reshape(4, 64, size)

    partial(oc, store_out)
    copy = push("core", 0, part_out, part_in, other)
    partial(c, store_own)
    copy.wait_recv()
    copies = []
    for d in (2, 1, 3):
        k = (zh + d) % 4
        red_out[d] = (part_own[k] + part_in[k]).astype(BF16)
        copies.append(push("rz", d, red_out.at[d], red_in.at[d], at_h(d)))
    total = part_own[zh] + part_in[zh]
    for copy in copies:
        copy.wait_recv()
    for d in (1, 2, 3):
        total = total + red_in[d].astype(F32)

    proj_in = total[:, 768:832].astype(BF16)
    proj_grad = total[:, 832:896].astype(BF16)
    v = total[:, :384] + scaling * nn(proj_in, upin_ref[...])
    grad = total[:, 384:768] + scaling * nn(proj_grad, dout_ref[...])
    t = jnp.tanh(coef * (v + 0.044715 * v * v * v))
    act = (0.5 * v * (1.0 + t)).astype(BF16)
    slope = 0.5 * (1.0 + t) + 0.5 * v * (1.0 - t * t) * coef * (1.0 + 3.0 * 0.044715 * v * v)
    pre_own = (grad * slope).astype(BF16)

    pre[c, zh] = pre_own
    mine = pre.at[c, zh]
    pz = {d: push("pz", d, mine, mine, at_h(d)) for d in (2, 1, 3)}
    pc = [push("pc", 0, mine, mine, other)]

    fxb[x] = jnp.concatenate([nt(act, dout_ref[...]), nt(pre_own, upin_ref[...])], 1)
    fx = [push("fx", d, fxb.at[x], fxb.at[x], at_x(d)) for d in (2, 1, 3)]
    eown[0] = scaling * tn(proj_in, pre_own)
    eown[1] = scaling * tn(proj_grad, act)
    ec = push("ec", 0, eown.at[oc], ein, other)

    for copy in fx:
        copy.wait_recv()
    fyb[y] = fxb[0] + fxb[1] + fxb[2] + fxb[3]
    fy = [push("fy", d, fyb.at[y], fyb.at[y], at_y(d)) for d in (2, 1, 3)]

    ec.wait_recv()
    esum = eown[c] + ein[...]
    ezout[...] = esum.astype(BF16).reshape(4, 16, 384)
    ez = [push("ez", d, ezout.at[(zh + d) % 4], ezin.at[d], at_h(d)) for d in (2, 1, 3)]

    for copy in fy:
        copy.wait_recv()
    fzb[z] = fyb[0] + fyb[1] + fyb[2] + fyb[3]
    fz = [push("fz", d, fzb.at[z], fzb.at[z], at_z(d)) for d in (2, 1, 3)]

    for d in (1, 3, 2):
        pz[d].wait_recv()
        got = pre.at[c, (zh + 4 - d) % 4]
        pc.append(push("pc", d, got, got, other))

    for copy in fz:
        copy.wait_recv()
    proj[c, zh] = (fzb[0] + fzb[1] + fzb[2] + fzb[3]).astype(BF16)
    mine = proj.at[c, zh]
    nz = {d: push("nz", d, mine, mine, at_h(d)) for d in (2, 1, 3)}
    nc = [push("nc", 0, mine, mine, other)]

    for copy in pc:
        copy.wait_recv()
    for h in range(2):
        rows = pre[h].reshape(256, 384)
        dxp[h] = nt(rows, w1[...]).astype(BF16).reshape(4, 4, 16, 768)
    c1 = []
    for d in (2, 1, 3):
        c1.append(push("ya", d, dxp.at[0, (y + d) % 4], c1in.at[0, d], at_y(d)))
        c1.append(push("xb", d, dxp.at[1, (x + d) % 4], c1in.at[1, d], at_x(d)))

    for copy in ez:
        copy.wait_recv()
    esl = ezout[zh].astype(F32)
    for d in (1, 2, 3):
        esl = esl + ezin[d].astype(F32)
    egb[c, zh] = esl.astype(BF16)
    mine = egb.at[c, zh]
    eg = {d: push("eg", d, mine, mine, at_h(d)) for d in (2, 1, 3)}
    eh = [push("eh", 0, mine, mine, other)]

    for copy in c1:
        copy.wait_recv()
    c2 = []
    s0 = dxp[0, y].astype(F32)
    s1 = dxp[1, x].astype(F32)
    for d in (1, 2, 3):
        s0 = s0 + c1in[0, d].astype(F32)
        s1 = s1 + c1in[1, d].astype(F32)
    c2out[0] = s0
    c2out[1] = s1
    for d in (2, 1, 3):
        c2.append(push("xa", d, c2out.at[0, (x + d) % 4], c2in.at[0, d], at_x(d)))
        c2.append(push("yb", d, c2out.at[1, (y + d) % 4], c2in.at[1, d], at_y(d)))

    for d in (1, 3, 2):
        nz[d].wait_recv()
        got = proj.at[c, (zh + 4 - d) % 4]
        nc.append(push("nc", d, got, got, other))

    for copy in c2:
        copy.wait_recv()
    s0 = c2out[0, x]
    s1 = c2out[1, y]
    for d in (1, 2, 3):
        s0 = s0 + c2in[0, d]
        s1 = s1 + c2in[1, d]
    czout[0] = s0[:8]
    czout[1] = s0[8:]
    czout[2] = s1[:8]
    czout[3] = s1[8:]
    cz = [push("cz", d, czout.at[(z + d) % 4], czin.at[d], at_z(d)) for d in (2, 1, 3)]

    for d in (1, 3, 2):
        eg[d].wait_recv()
        got = egb.at[c, (zh + 4 - d) % 4]
        eh.append(push("eh", d, got, got, other))

    for copy in nc:
        copy.wait_recv()
    rank = proj[...].reshape(512, 128)
    xs = strip[:, :, 0].reshape(512, 768)
    gs = strip[:, :, 1].reshape(512, 768)
    gupout_ref[...] = scaling * tn(rank[:, :64], gs)
    gdin_ref[...] = scaling * tn(rank[:, 64:], xs)

    for copy in eh:
        copy.wait_recv()
    gupin_ref[...] = egb[0].reshape(64, 384).astype(F32)
    gdout_ref[...] = egb[1].reshape(64, 384).astype(F32)

    half = z // 2
    k = jnp.where(half == 0, y, x)
    j = jnp.where(half == 0, x, y)
    rows = proj[half, k, pl.ds(pl.multiple_of(j * 16, 16), 16), :].astype(F32)
    back = jnp.where(z % 2 == 0, rows[:8], rows[8:])[:, 64:].astype(BF16)
    extra = scaling * nn(back, din_ref[...])
    for copy in cz:
        copy.wait_recv()
    out = czout[z] + extra
    for d in (1, 2, 3):
        out = out + czin[d]
    dx_ref[...] = out.astype(BF16)

    for copy in sent:
        copy.wait_send()


def hand_over(*refs):
    ins, outs, held, sems = refs[:5], refs[5:10], refs[10:15], refs[15]
    reads = [pltpu.make_async_copy(ins[i], held[i], sems.at[0, i]) for i in range(5)]
    writes = [pltpu.make_async_copy(held[i], outs[i], sems.at[1, i]) for i in range(5)]
    for copy in reads:
        copy.start()
    for read, write in zip(reads, writes):
        read.wait()
        write.start()
    for copy in writes:
        copy.wait()


def shards(x, g, w1, w2, din, upin, dout, upout):
    vmem = pl.BlockSpec(memory_space=pltpu.VMEM)
    hbm = pl.BlockSpec(memory_space=pl.ANY)
    nf = len(FAMILIES)
    shapes = (
        jax.ShapeDtypeStruct((8, 768), BF16),
        jax.ShapeDtypeStruct((64, 768), F32),
        jax.ShapeDtypeStruct((64, 384), F32),
        jax.ShapeDtypeStruct((64, 384), F32),
        jax.ShapeDtypeStruct((64, 768), F32),
    )
    made = pl.pallas_call(
        kernel,
        out_shape=shapes,
        in_specs=[hbm] * 8,
        out_specs=(vmem,) * 5,
        scratch_shapes=[
            pltpu.VMEM((8, 768), BF16),
            pltpu.VMEM((8, 768), BF16),
            pltpu.VMEM((768, 384), BF16),
            pltpu.VMEM((384, 768), BF16),
            pltpu.VMEM((64, 768), BF16),
            pltpu.VMEM((64, 384), BF16),
            pltpu.VMEM((64, 384), BF16),
            pltpu.VMEM((64, 768), BF16),
            pltpu.VMEM((4, 16, 768), BF16),
            pltpu.VMEM((2, 4, 2, 4, 16, 768), BF16),
            pltpu.VMEM((4, 64, 896), F32),
            pltpu.VMEM((4, 64, 896), F32),
            pltpu.VMEM((4, 64, 896), F32),
            pltpu.VMEM((4, 64, 896), BF16),
            pltpu.VMEM((4, 64, 896), BF16),
            pltpu.VMEM((2, 4, 64, 384), BF16),
            pltpu.VMEM((2, 4, 64, 128), BF16),
            pltpu.VMEM((4, 64, 128), F32),
            pltpu.VMEM((4, 64, 128), F32),
            pltpu.VMEM((4, 64, 128), F32),
            pltpu.VMEM((2, 64, 384), F32),
            pltpu.VMEM((64, 384), F32),
            pltpu.VMEM((4, 16, 384), BF16),
            pltpu.VMEM((4, 16, 384), BF16),
            pltpu.VMEM((2, 4, 16, 384), BF16),
            pltpu.VMEM((2, 4, 4, 16, 768), BF16),
            pltpu.VMEM((2, 4, 4, 16, 768), BF16),
            pltpu.VMEM((2, 4, 16, 768), F32),
            pltpu.VMEM((2, 4, 16, 768), F32),
            pltpu.VMEM((4, 8, 768), F32),
            pltpu.VMEM((4, 8, 768), F32),
            pltpu.SemaphoreType.DMA((8,)),
            pltpu.SemaphoreType.DMA((nf, 4)),
            pltpu.SemaphoreType.DMA((nf, 4)),
        ],
        compiler_params=pltpu.CompilerParams(
            collective_id=0, has_side_effects=True, vmem_limit_bytes=60 * 1024 * 1024
        ),
    )(x, g, w1, w2, din, upin, dout, upout)
    return pl.pallas_call(
        hand_over,
        out_shape=shapes,
        in_specs=[hbm] * 5,
        out_specs=(hbm,) * 5,
        scratch_shapes=[pltpu.VMEM(t.shape, t.dtype) for t in shapes]
        + [pltpu.SemaphoreType.DMA((2, 5))],
        compiler_params=pltpu.CompilerParams(vmem_limit_bytes=60 * 1024 * 1024),
    )(*made)


def solution(mesh):
    return jax.shard_map(
        shards,
        mesh=mesh,
        in_specs=(
            P("wide", "narrow"),
            P("wide", "narrow"),
            P("narrow", "wide"),
            P("wide", "narrow"),
            P(None, "narrow"),
            P(None, "wide"),
            P(None, "wide"),
            P(None, "narrow"),
        ),
        out_specs=(
            P("wide", "narrow"),
            P(None, "narrow"),
            P(None, "wide"),
            P(None, "wide"),
            P(None, "narrow"),
        ),
        check_vma=False,
    )
```

```python
import functools
import math

import jax
import jax.numpy as jnp
from jax import lax
from jax.experimental import pallas as pl
from jax.experimental.pallas import tpu as pltpu
from jax.sharding import PartitionSpec as P

MESH = pl.DeviceIdType.MESH
F32 = jnp.float32
BF16 = jnp.bfloat16
scaling = 2.0
coef = math.sqrt(2.0 / math.pi)

FAMILIES = (
    "gz", "ga", "gb", "gc", "gd", "core", "cj", "rz0", "rz1", "rz2", "rz3", "rj", "pj",
    "pz0", "pz1", "pz2", "pz3", "pc0", "pc1", "pc2", "pc3", "fx", "fy", "fz", "nz", "nc",
    "ec", "ez", "eg", "eh", "ya", "xa", "xb", "yb", "cz",
)
FAMILY = {name: i for i, name in enumerate(FAMILIES)}
ORDER = (0, 1, 3, 2)


def nn(left, right):
    return lax.dot_general(left, right, (((1,), (0,)), ((), ())), preferred_element_type=F32)


def nt(left, right):
    return lax.dot_general(left, right, (((1,), (1,)), ((), ())), preferred_element_type=F32)


def tn(left, right):
    return lax.dot_general(left, right, (((0,), (0,)), ((), ())), preferred_element_type=F32)


def kernel(
    x_hbm, g_hbm, w1_hbm, w2_hbm, din_hbm, upin_hbm, dout_hbm, upout_hbm,
    dx_ref, gdin_ref, gupin_ref, gdout_ref, gupout_ref,
    x_ref, g_ref, w1, w2, din_ref, upin_ref, dout_ref, upout_ref,
    zbuf, strip, part, part_in, pj, pj_in, red_out, red_in, pj_out, pj_red, pj_all,
    act_all, pre, proj, fxb, fyb, fzb, eown, ein, ezout, ezin, egb,
    dxp, c1in, c2out, c2in, czout, czin,
    wsem, ssem, rsem,
):
    w = lax.axis_index("wide")
    n = lax.axis_index("narrow")
    y, z, x = w // 16, (w // 4) % 4, w % 4
    zh, c = n // 2, n % 2
    oc = 1 - c

    def at_x(d):
        return (y * 16 + z * 4 + (x + d) % 4, n)

    def at_y(d):
        return (((y + d) % 4) * 16 + z * 4 + x, n)

    def at_z(d):
        return (y * 16 + ((z + d) % 4) * 4 + x, n)

    def at_h(d):
        return (w, ((zh + d) % 4) * 2 + c)

    other = (w, zh * 2 + oc)
    sent = []

    def push(family, slot, src, dst, to):
        i = FAMILY[family]
        copy = pltpu.make_async_remote_copy(
            src_ref=src, dst_ref=dst, send_sem=ssem.at[i, slot], recv_sem=rsem.at[i, slot],
            device_id=to, device_id_type=MESH,
        )
        copy.start()
        sent.append(copy)
        return copy

    loads = [
        pltpu.make_async_copy(src, dst, wsem.at[i])
        for i, (src, dst) in enumerate((
            (x_hbm, x_ref), (g_hbm, g_ref), (w1_hbm, w1), (w2_hbm, w2), (din_hbm, din_ref),
            (upin_hbm, upin_ref), (dout_hbm, dout_ref), (upout_hbm, upout_ref),
        ))
    ]
    for load in loads:
        load.start()

    barrier = pltpu.get_barrier_semaphore()
    for d in (1, 2, 3):
        for at in (at_x, at_y, at_z, at_h):
            pl.semaphore_signal(barrier, inc=1, device_id=at(d), device_id_type=MESH)
    pl.semaphore_signal(barrier, inc=1, device_id=other, device_id_type=MESH)

    loads[0].wait()
    loads[1].wait()
    zbuf[z] = jnp.concatenate([x_ref[...].astype(F32), g_ref[...].astype(F32)], 0).astype(BF16)
    pl.semaphore_wait(barrier, 13)

    copies = [push("gz", d, zbuf.at[z], zbuf.at[z], at_z(d)) for d in (2, 1, 3)]
    for copy in copies:
        copy.wait_recv()
    planes = [zbuf[i].astype(F32) for i in range(4)]
    for t in range(2):
        rows = slice(8 * t, 8 * t + 8)
        strip[0, y, t, x] = jnp.concatenate([planes[0][rows], planes[1][rows]], 0).astype(BF16)
        strip[1, x, t, y] = jnp.concatenate([planes[2][rows], planes[3][rows]], 0).astype(BF16)
    copies = []
    for d in (2, 1, 3):
        mine = strip.at[0, y, :, x]
        copies.append(push("ga", d, mine, mine, at_x(d)))
        mine = strip.at[1, x, :, y]
        copies.append(push("gb", d, mine, mine, at_y(d)))
    for copy in copies:
        copy.wait_recv()
    gc, gd = {}, {}
    for d in (1, 3, 2):
        mine = strip.at[0, y]
        gc[d] = push("gc", d, mine, mine, at_y(d))
        mine = strip.at[1, x]
        gd[d] = push("gd", d, mine, mine, at_x(d))
    for load in loads[2:]:
        load.wait()

    core = {}

    def multiply(d):
        if d:
            gc[d].wait_recv()
            gd[d].wait_recv()
        ka, kb = (y + 4 - d) % 4, (x + 4 - d) % 4
        xs = jnp.concatenate([strip[0, ka, 0].reshape(64, 768), strip[1, kb, 0].reshape(64, 768)], 0)
        gs = jnp.concatenate([strip[0, ka, 1].reshape(64, 768), strip[1, kb, 1].reshape(64, 768)], 0)
        hp = nn(xs, w1[...])
        bp = nt(gs, w2[...])
        for h in range(2):
            rows = slice(64 * h, 64 * h + 64)
            part[d, h, :, :, :384] = hp[rows].reshape(4, 16, 384)
            part[d, h, :, :, 384:] = bp[rows].reshape(4, 16, 384)
        core[d] = push("core", d, part.at[d, oc], part_in.at[d], other)
        if d == 0:
            both = jnp.concatenate([nt(xs, din_ref[...]), nt(gs, upout_ref[...])], 1)
            pj[...] = both.reshape(2, 4, 16, 128)
            core["j"] = push("cj", 0, pj.at[oc], pj_in, other)

    rz = {}

    def scatter(d):
        core[d].wait_recv()
        red_out[d] = (part[d, c] + part_in[d]).astype(BF16)
        rz[d] = [
            push("rz%d" % d, e, red_out.at[d, (zh + e) % 4], red_in.at[e, d], at_h(e))
            for e in (2, 1, 3)
        ]
        if d == 0:
            core["j"].wait_recv()
            pj_out[...] = (pj[c] + pj_in[...]).astype(BF16)
            rz["j"] = [
                push("rj", e, pj_out.at[(zh + e) % 4], pj_red.at[e], at_h(e)) for e in (2, 1, 3)
            ]

    for d in ORDER:
        multiply(d)
        scatter(d)

    for copy in rz["j"]:
        copy.wait_recv()
    total = pj[c, zh] + pj_in[zh]
    for e in (1, 2, 3):
        total = total + pj_red[e].astype(F32)
    pj_all[0] = total.astype(BF16)
    pjc = {}
    for d in (2, 1, 3):
        to = (oc * at_y(d)[0] + c * at_x(d)[0], n)
        pjc[d] = push("pj", d, pj_all.at[0], pj_all.at[d], to)

    pz, pc = {}, {}

    def activate(d):
        for copy in rz[d]:
            copy.wait_recv()
        if d:
            pjc[d].wait_recv()
        total = part[d, c, zh] + part_in[d, zh]
        for e in (1, 2, 3):
            total = total + red_in[e, d].astype(F32)
        both = pj_all[d]
        v = total[:, :384] + scaling * nn(both[:, :64], upin_ref[...])
        grad = total[:, 384:] + scaling * nn(both[:, 64:], dout_ref[...])
        t = jnp.tanh(coef * (v + 0.044715 * v * v * v))
        act_all[d] = (0.5 * v * (1.0 + t)).astype(BF16)
        slope = 0.5 * (1.0 + t) + 0.5 * v * (1.0 - t * t) * coef * (1.0 + 3.0 * 0.044715 * v * v)
        pre[c, zh, d] = (grad * slope).astype(BF16)
        mine = pre.at[c, zh, d]
        pz[d] = {e: push("pz%d" % d, e, mine, mine, at_h(e)) for e in (2, 1, 3)}
        pc[d] = [push("pc%d" % d, 0, mine, mine, other)]

    def forward(d):
        for e in (1, 3, 2):
            pz[d][e].wait_recv()
            got = pre.at[c, (zh + 4 - e) % 4, d]
            pc[d].append(push("pc%d" % d, e, got, got, other))

    c1 = []

    def back(d):
        for copy in pc[d]:
            copy.wait_recv()
        rows = jnp.concatenate([pre[0, :, d].reshape(64, 384), pre[1, :, d].reshape(64, 384)], 0)
        value = nt(rows, w1[...]).astype(BF16)
        dxp[0, d] = value[:64].reshape(4, 16, 768)
        dxp[1, d] = value[64:].reshape(4, 16, 768)
        if d:
            e = 4 - d
            c1.append(push("ya", e, dxp.at[0, d], c1in.at[0, e], at_y(e)))
            c1.append(push("xb", e, dxp.at[1, d], c1in.at[1, e], at_x(e)))

    for d in ORDER:
        activate(d)

    acts = act_all[...].reshape(64, 384)
    pres = pre[c, zh].reshape(64, 384)
    both = jnp.concatenate([nt(acts, dout_ref[...]), nt(pres, upin_ref[...])], 1).reshape(4, 16, 128)
    for d in range(4):
        fxb[x, oc * ((y + 4 - d) % 4) + c * ((x + 4 - d) % 4)] = both[d]
    fx = [push("fx", d, fxb.at[x], fxb.at[x], at_x(d)) for d in (2, 1, 3)]
    forward(0)
    ranks = pj_all[...].reshape(64, 128)
    eown[0] = scaling * tn(ranks[:, :64], pres)
    eown[1] = scaling * tn(ranks[:, 64:], acts)
    ec = push("ec", 0, eown.at[oc], ein, other)
    forward(1)
    for copy in fx:
        copy.wait_recv()
    fyb[y] = fxb[0] + fxb[1] + fxb[2] + fxb[3]
    fy = [push("fy", d, fyb.at[y], fyb.at[y], at_y(d)) for d in (2, 1, 3)]
    forward(3)
    back(0)
    ec.wait_recv()
    ezout[...] = (eown[c] + ein[...]).astype(BF16).reshape(4, 16, 384)
    ez = [push("ez", d, ezout.at[(zh + d) % 4], ezin.at[d], at_h(d)) for d in (2, 1, 3)]
    back(1)
    for copy in fy:
        copy.wait_recv()
    fzb[z] = fyb[0] + fyb[1] + fyb[2] + fyb[3]
    fz = [push("fz", d, fzb.at[z], fzb.at[z], at_z(d)) for d in (2, 1, 3)]
    forward(2)
    back(3)
    back(2)

    for copy in fz:
        copy.wait_recv()
    proj[c, :, zh] = (fzb[0] + fzb[1] + fzb[2] + fzb[3]).astype(BF16)
    mine = proj.at[c, :, zh]
    nz = {d: push("nz", d, mine, mine, at_h(d)) for d in (2, 1, 3)}
    nc = [push("nc", 0, mine, mine, other)]

    for copy in ez:
        copy.wait_recv()
    esl = ezout[zh].astype(F32)
    for d in (1, 2, 3):
        esl = esl + ezin[d].astype(F32)
    egb[c, zh] = esl.astype(BF16)
    mine = egb.at[c, zh]
    eg = {d: push("eg", d, mine, mine, at_h(d)) for d in (2, 1, 3)}
    eh = [push("eh", 0, mine, mine, other)]

    for copy in c1:
        copy.wait_recv()
    c2 = []
    s0 = dxp[0, 0].astype(F32)
    s1 = dxp[1, 0].astype(F32)
    for d in (1, 2, 3):
        s0 = s0 + c1in[0, d].astype(F32)
        s1 = s1 + c1in[1, d].astype(F32)
    c2out[0] = s0
    c2out[1] = s1
    for d in (2, 1, 3):
        c2.append(push("xa", d, c2out.at[0, (x + d) % 4], c2in.at[0, d], at_x(d)))
        c2.append(push("yb", d, c2out.at[1, (y + d) % 4], c2in.at[1, d], at_y(d)))

    for d in (1, 3, 2):
        nz[d].wait_recv()
        got = proj.at[c, :, (zh + 4 - d) % 4]
        nc.append(push("nc", d, got, got, other))

    for copy in c2:
        copy.wait_recv()
    s0 = c2out[0, x]
    s1 = c2out[1, y]
    for d in (1, 2, 3):
        s0 = s0 + c2in[0, d]
        s1 = s1 + c2in[1, d]
    czout[0] = s0[:8]
    czout[1] = s0[8:]
    czout[2] = s1[:8]
    czout[3] = s1[8:]
    cz = [push("cz", d, czout.at[(z + d) % 4], czin.at[d], at_z(d)) for d in (2, 1, 3)]

    for d in (1, 3, 2):
        eg[d].wait_recv()
        got = egb.at[c, (zh + 4 - d) % 4]
        eh.append(push("eh", d, got, got, other))

    for copy in nc:
        copy.wait_recv()
    rank = proj[...].reshape(512, 128)
    xs = strip[:, :, 0].reshape(512, 768)
    gs = strip[:, :, 1].reshape(512, 768)
    gupout_ref[...] = scaling * tn(rank[:, :64], gs)
    gdin_ref[...] = scaling * tn(rank[:, 64:], xs)

    for copy in eh:
        copy.wait_recv()
    gupin_ref[...] = egb[0].reshape(64, 384).astype(F32)
    gdout_ref[...] = egb[1].reshape(64, 384).astype(F32)

    half = z // 2
    k = (1 - half) * y + half * x
    j = (1 - half) * x + half * y
    rows = proj[half, k, j].astype(F32)
    own = jnp.where(z % 2 == 0, rows[:8], rows[8:])[:, 64:].astype(BF16)
    extra = scaling * nn(own, din_ref[...])
    for copy in cz:
        copy.wait_recv()
    out = czout[z] + extra
    for d in (1, 2, 3):
        out = out + czin[d]
    dx_ref[...] = out.astype(BF16)

    for copy in sent:
        copy.wait_send()


def hand_over(*refs):
    ins, outs, held, sems = refs[:5], refs[5:10], refs[10:15], refs[15]
    reads = [pltpu.make_async_copy(ins[i], held[i], sems.at[0, i]) for i in range(5)]
    writes = [pltpu.make_async_copy(held[i], outs[i], sems.at[1, i]) for i in range(5)]
    for copy in reads:
        copy.start()
    for read, write in zip(reads, writes):
        read.wait()
        write.start()
    for copy in writes:
        copy.wait()


def shards(x, g, w1, w2, din, upin, dout, upout):
    vmem = pl.BlockSpec(memory_space=pltpu.VMEM)
    hbm = pl.BlockSpec(memory_space=pl.ANY)
    nf = len(FAMILIES)
    shapes = (
        jax.ShapeDtypeStruct((8, 768), BF16),
        jax.ShapeDtypeStruct((64, 768), F32),
        jax.ShapeDtypeStruct((64, 384), F32),
        jax.ShapeDtypeStruct((64, 384), F32),
        jax.ShapeDtypeStruct((64, 768), F32),
    )
    made = pl.pallas_call(
        kernel,
        out_shape=shapes,
        in_specs=[hbm] * 8,
        out_specs=(vmem,) * 5,
        scratch_shapes=[
            pltpu.VMEM((8, 768), BF16),
            pltpu.VMEM((8, 768), BF16),
            pltpu.VMEM((768, 384), BF16),
            pltpu.VMEM((384, 768), BF16),
            pltpu.VMEM((64, 768), BF16),
            pltpu.VMEM((64, 384), BF16),
            pltpu.VMEM((64, 384), BF16),
            pltpu.VMEM((64, 768), BF16),
            pltpu.VMEM((4, 16, 768), BF16),
            pltpu.VMEM((2, 4, 2, 4, 16, 768), BF16),
            pltpu.VMEM((4, 2, 4, 16, 768), F32),
            pltpu.VMEM((4, 4, 16, 768), F32),
            pltpu.VMEM((2, 4, 16, 128), F32),
            pltpu.VMEM((4, 16, 128), F32),
            pltpu.VMEM((4, 4, 16, 768), BF16),
            pltpu.VMEM((4, 4, 16, 768), BF16),
            pltpu.VMEM((4, 16, 128), BF16),
            pltpu.VMEM((4, 16, 128), BF16),
            pltpu.VMEM((4, 16, 128), BF16),
            pltpu.VMEM((4, 16, 384), BF16),
            pltpu.VMEM((2, 4, 4, 16, 384), BF16),
            pltpu.VMEM((2, 4, 4, 16, 128), BF16),
            pltpu.VMEM((4, 4, 16, 128), F32),
            pltpu.VMEM((4, 4, 16, 128), F32),
            pltpu.VMEM((4, 4, 16, 128), F32),
            pltpu.VMEM((2, 64, 384), F32),
            pltpu.VMEM((64, 384), F32),
            pltpu.VMEM((4, 16, 384), BF16),
            pltpu.VMEM((4, 16, 384), BF16),
            pltpu.VMEM((2, 4, 16, 384), BF16),
            pltpu.VMEM((2, 4, 4, 16, 768), BF16),
            pltpu.VMEM((2, 4, 4, 16, 768), BF16),
            pltpu.VMEM((2, 4, 16, 768), F32),
            pltpu.VMEM((2, 4, 16, 768), F32),
            pltpu.VMEM((4, 8, 768), F32),
            pltpu.VMEM((4, 8, 768), F32),
            pltpu.SemaphoreType.DMA((8,)),
            pltpu.SemaphoreType.DMA((nf, 4)),
            pltpu.SemaphoreType.DMA((nf, 4)),
        ],
        compiler_params=pltpu.CompilerParams(
            collective_id=0, has_side_effects=True, vmem_limit_bytes=60 * 1024 * 1024
        ),
    )(x, g, w1, w2, din, upin, dout, upout)
    return pl.pallas_call(
        hand_over,
        out_shape=shapes,
        in_specs=[hbm] * 5,
        out_specs=(hbm,) * 5,
        scratch_shapes=[pltpu.VMEM(t.shape, t.dtype) for t in shapes]
        + [pltpu.SemaphoreType.DMA((2, 5))],
        compiler_params=pltpu.CompilerParams(vmem_limit_bytes=60 * 1024 * 1024),
    )(*made)


def solution(mesh):
    return jax.shard_map(
        shards,
        mesh=mesh,
        in_specs=(
            P("wide", "narrow"),
            P("wide", "narrow"),
            P("narrow", "wide"),
            P("wide", "narrow"),
            P(None, "narrow"),
            P(None, "wide"),
            P(None, "wide"),
            P(None, "narrow"),
        ),
        out_specs=(
            P("wide", "narrow"),
            P(None, "narrow"),
            P(None, "wide"),
            P(None, "wide"),
            P(None, "narrow"),
        ),
        check_vma=False,
    )
```

```python
import functools
import math

import jax
import jax.numpy as jnp
from jax import lax
from jax.experimental import pallas as pl
from jax.experimental.pallas import tpu as pltpu
from jax.sharding import PartitionSpec as P

MESH = pl.DeviceIdType.MESH
F32 = jnp.float32
BF16 = jnp.bfloat16
scaling = 2.0
coef = math.sqrt(2.0 / math.pi)

FAMILIES = (
    "gz", "ga", "gb", "gc", "gd", "gf", "gh", "core", "cj", "rz0", "rz1", "rz2", "rz3", "rj", "pj",
    "pz0", "pz1", "pz2", "pz3", "pc0", "pc1", "pc2", "pc3", "fx", "fy", "fz", "nz", "nc",
    "ec", "ez", "eg", "eh", "ya", "xa", "xb", "yb", "cz",
)
FAMILY = {name: i for i, name in enumerate(FAMILIES)}
ORDER = (0, 1, 3, 2)


def nn(left, right):
    return lax.dot_general(left, right, (((1,), (0,)), ((), ())), preferred_element_type=F32)


def nt(left, right):
    return lax.dot_general(left, right, (((1,), (1,)), ((), ())), preferred_element_type=F32)


def tn(left, right):
    return lax.dot_general(left, right, (((0,), (0,)), ((), ())), preferred_element_type=F32)


def kernel(
    x_hbm, g_hbm, w1_hbm, w2_hbm, din_hbm, upin_hbm, dout_hbm, upout_hbm,
    dx_hbm, gdin_hbm, gupin_hbm, gdout_hbm, gupout_hbm,
    x_ref, g_ref, w1, w2, din_ref, upin_ref, dout_ref, upout_ref,
    zbuf, strip, part, part_in, pj, pj_in, red_out, red_in, pj_out, pj_red, pj_all,
    act_all, pre, proj, fxb, fyb, fzb, eown, ein, ezout, ezin, egb,
    dxp, c1in, c2out, c2in, czout, czin,
    dx_ref, gdin_ref, gupin_ref, gdout_ref, gupout_ref, wsem, osem, ssem, rsem,
):
    w = lax.axis_index("wide")
    n = lax.axis_index("narrow")
    y, z, x = w // 16, (w // 4) % 4, w % 4
    zh, c = n // 2, n % 2
    oc = 1 - c

    def at_x(d):
        return (y * 16 + z * 4 + (x + d) % 4, n)

    def at_y(d):
        return (((y + d) % 4) * 16 + z * 4 + x, n)

    def at_z(d):
        return (y * 16 + ((z + d) % 4) * 4 + x, n)

    def at_h(d):
        return (w, ((zh + d) % 4) * 2 + c)

    other = (w, zh * 2 + oc)
    sent = []

    def drain():
        while sent:
            sent.pop(0).wait_send()

    def push(family, slot, src, dst, to):
        i = FAMILY[family]
        copy = pltpu.make_async_remote_copy(
            src_ref=src, dst_ref=dst, send_sem=ssem.at[i, slot], recv_sem=rsem.at[i, slot],
            device_id=to, device_id_type=MESH,
        )
        copy.start()
        sent.append(copy)
        return copy

    outs = []

    def save(i, src, dst):
        copy = pltpu.make_async_copy(src, dst, osem.at[i])
        copy.start()
        outs.append(copy)

    loads = [
        pltpu.make_async_copy(src, dst, wsem.at[i])
        for i, (src, dst) in enumerate((
            (x_hbm, x_ref), (g_hbm, g_ref), (w1_hbm, w1), (w2_hbm, w2), (din_hbm, din_ref),
            (upin_hbm, upin_ref), (dout_hbm, dout_ref), (upout_hbm, upout_ref),
        ))
    ]
    for load in loads:
        load.start()

    barrier = pltpu.get_barrier_semaphore()
    for d in (1, 2, 3):
        for at in (at_x, at_y, at_z, at_h):
            pl.semaphore_signal(barrier, inc=1, device_id=at(d), device_id_type=MESH)
    pl.semaphore_signal(barrier, inc=1, device_id=other, device_id_type=MESH)

    loads[0].wait()
    loads[1].wait()
    zbuf[z] = jnp.concatenate([x_ref[...].astype(F32), g_ref[...].astype(F32)], 0).astype(BF16)
    pl.semaphore_wait(barrier, 13)

    copies = [push("gz", d, zbuf.at[z], zbuf.at[z], at_z(d)) for d in (2, 1, 3)]
    for copy in copies:
        copy.wait_recv()
    planes = [zbuf[i].astype(F32) for i in range(4)]
    for t in range(2):
        rows = slice(8 * t, 8 * t + 8)
        strip[0, y, t, x] = jnp.concatenate([planes[0][rows], planes[1][rows]], 0).astype(BF16)
        strip[1, x, t, y] = jnp.concatenate([planes[2][rows], planes[3][rows]], 0).astype(BF16)
    copies = []
    for d in (2, 1, 3):
        mine = strip.at[0, y, :, x]
        copies.append(push("ga", d, mine, mine, at_x(d)))
        mine = strip.at[1, x, :, y]
        copies.append(push("gb", d, mine, mine, at_y(d)))
    for copy in copies:
        copy.wait_recv()
    gc, gd = {}, {}
    for d in (1, 3):
        mine = strip.at[0, y]
        gc[d] = push("gc", d, mine, mine, at_y(d))
        mine = strip.at[1, x]
        gd[d] = push("gd", d, mine, mine, at_x(d))
    for load in loads[2:]:
        load.wait()

    core = {}

    def multiply(d):
        ka, kb = (y + 4 - d) % 4, (x + 4 - d) % 4
        xs = jnp.concatenate([strip[0, ka, 0].reshape(64, 768), strip[1, kb, 0].reshape(64, 768)], 0)
        gs = jnp.concatenate([strip[0, ka, 1].reshape(64, 768), strip[1, kb, 1].reshape(64, 768)], 0)
        hp = nn(xs, w1[...])
        bp = nt(gs, w2[...])
        for h in range(2):
            rows = slice(64 * h, 64 * h + 64)
            part[d, h, :, :, :384] = hp[rows].reshape(4, 16, 384)
            part[d, h, :, :, 384:] = bp[rows].reshape(4, 16, 384)
        core[d] = push("core", d, part.at[d, oc], part_in.at[d], other)
        if d == 0:
            both = jnp.concatenate([nt(xs, din_ref[...]), nt(gs, upout_ref[...])], 1)
            pj[...] = both.reshape(2, 4, 16, 128)
            core["j"] = push("cj", 0, pj.at[oc], pj_in, other)

    rz = {}

    def scatter(d):
        core[d].wait_recv()
        red_out[d] = (part[d, c] + part_in[d]).astype(BF16)
        rz[d] = [
            push("rz%d" % d, e, red_out.at[d, (zh + e) % 4], red_in.at[e, d], at_h(e))
            for e in (2, 1, 3)
        ]
        if d == 0:
            core["j"].wait_recv()
            pj_out[...] = (pj[c] + pj_in[...]).astype(BF16)
            rz["j"] = [
                push("rj", e, pj_out.at[(zh + e) % 4], pj_red.at[e], at_h(e)) for e in (2, 1, 3)
            ]

    multiply(0)
    scatter(0)
    far = []
    for t, d in ((0, 1), (1, 3)):
        gc[d].wait_recv()
        got = strip.at[0, (y + 4 - d) % 4, t]
        far.append(push("gf", d, got, got, at_y(d)))
        gd[d].wait_recv()
        got = strip.at[1, (x + 4 - d) % 4, t]
        far.append(push("gh", d, got, got, at_x(d)))
    multiply(1)
    multiply(3)
    scatter(1)
    scatter(3)
    for copy in far:
        copy.wait_recv()
    multiply(2)
    for copy in rz["j"]:
        copy.wait_recv()
    total = pj[c, zh] + pj_in[zh]
    for e in (1, 2, 3):
        total = total + pj_red[e].astype(F32)
    pj_all[0] = total.astype(BF16)
    pjc = {}
    for d in (2, 1, 3):
        to = (oc * at_y(d)[0] + c * at_x(d)[0], n)
        pjc[d] = push("pj", d, pj_all.at[0], pj_all.at[d], to)
    scatter(2)

    pz, pc = {}, {}

    def activate(d):
        for copy in rz[d]:
            copy.wait_recv()
        if d:
            pjc[d].wait_recv()
        total = part[d, c, zh] + part_in[d, zh]
        for e in (1, 2, 3):
            total = total + red_in[e, d].astype(F32)
        both = pj_all[d]
        v = total[:, :384] + scaling * nn(both[:, :64], upin_ref[...])
        grad = total[:, 384:] + scaling * nn(both[:, 64:], dout_ref[...])
        t = jnp.tanh(coef * (v + 0.044715 * v * v * v))
        act_all[d] = (0.5 * v * (1.0 + t)).astype(BF16)
        slope = 0.5 * (1.0 + t) + 0.5 * v * (1.0 - t * t) * coef * (1.0 + 3.0 * 0.044715 * v * v)
        pre[c, zh, d] = (grad * slope).astype(BF16)
        mine = pre.at[c, zh, d]
        pz[d] = {e: push("pz%d" % d, e, mine, mine, at_h(e)) for e in (2, 1, 3)}
        pc[d] = [push("pc%d" % d, 0, mine, mine, other)]

    def forward(d):
        for e in (1, 3, 2):
            pz[d][e].wait_recv()
            got = pre.at[c, (zh + 4 - e) % 4, d]
            pc[d].append(push("pc%d" % d, e, got, got, other))

    c1 = []

    def back(d):
        for copy in pc[d]:
            copy.wait_recv()
        rows = jnp.concatenate([pre[0, :, d].reshape(64, 384), pre[1, :, d].reshape(64, 384)], 0)
        value = nt(rows, w1[...]).astype(BF16)
        dxp[0, d] = value[:64].reshape(4, 16, 768)
        dxp[1, d] = value[64:].reshape(4, 16, 768)
        if d:
            e = 4 - d
            c1.append(push("ya", e, dxp.at[0, d], c1in.at[0, e], at_y(e)))
            c1.append(push("xb", e, dxp.at[1, d], c1in.at[1, e], at_x(e)))

    for d in ORDER:
        activate(d)

    acts = act_all[...].reshape(64, 384)
    pres = pre[c, zh].reshape(64, 384)
    both = jnp.concatenate([nt(acts, dout_ref[...]), nt(pres, upin_ref[...])], 1).reshape(4, 16, 128)
    for d in range(4):
        fxb[x, oc * ((y + 4 - d) % 4) + c * ((x + 4 - d) % 4)] = both[d]
    fx = [push("fx", d, fxb.at[x], fxb.at[x], at_x(d)) for d in (2, 1, 3)]
    ranks = pj_all[...].reshape(64, 128)
    eown[0] = scaling * tn(ranks[:, :64], pres)
    eown[1] = scaling * tn(ranks[:, 64:], acts)
    ec = push("ec", 0, eown.at[oc], ein, other)
    forward(0)
    for copy in fx:
        copy.wait_recv()
    fyb[y] = fxb[0] + fxb[1] + fxb[2] + fxb[3]
    fy = [push("fy", d, fyb.at[y], fyb.at[y], at_y(d)) for d in (2, 1, 3)]
    forward(1)
    back(0)
    ec.wait_recv()
    ezout[...] = (eown[c] + ein[...]).astype(BF16).reshape(4, 16, 384)
    ez = [push("ez", d, ezout.at[(zh + d) % 4], ezin.at[d], at_h(d)) for d in (2, 1, 3)]
    for copy in fy:
        copy.wait_recv()
    fzb[z] = fyb[0] + fyb[1] + fyb[2] + fyb[3]
    fz = [push("fz", d, fzb.at[z], fzb.at[z], at_z(d)) for d in (2, 1, 3)]
    forward(3)
    back(1)
    drain()
    forward(2)
    back(3)
    back(2)

    for copy in fz:
        copy.wait_recv()
    proj[c, :, zh] = (fzb[0] + fzb[1] + fzb[2] + fzb[3]).astype(BF16)
    mine = proj.at[c, :, zh]
    nz = {d: push("nz", d, mine, mine, at_h(d)) for d in (2, 1, 3)}
    nc = [push("nc", 0, mine, mine, other)]

    for copy in ez:
        copy.wait_recv()
    esl = ezout[zh].astype(F32)
    for d in (1, 2, 3):
        esl = esl + ezin[d].astype(F32)
    egb[c, zh] = esl.astype(BF16)
    mine = egb.at[c, zh]
    eg = {d: push("eg", d, mine, mine, at_h(d)) for d in (2, 1, 3)}
    eh = [push("eh", 0, mine, mine, other)]

    for copy in c1:
        copy.wait_recv()
    c2 = []
    s0 = dxp[0, 0].astype(F32)
    s1 = dxp[1, 0].astype(F32)
    for d in (1, 2, 3):
        s0 = s0 + c1in[0, d].astype(F32)
        s1 = s1 + c1in[1, d].astype(F32)
    c2out[0] = s0
    c2out[1] = s1
    for d in (2, 1, 3):
        c2.append(push("xa", d, c2out.at[0, (x + d) % 4], c2in.at[0, d], at_x(d)))
        c2.append(push("yb", d, c2out.at[1, (y + d) % 4], c2in.at[1, d], at_y(d)))

    for d in (1, 3, 2):
        nz[d].wait_recv()
        got = proj.at[c, :, (zh + 4 - d) % 4]
        nc.append(push("nc", d, got, got, other))

    for copy in c2:
        copy.wait_recv()
    s0 = c2out[0, x]
    s1 = c2out[1, y]
    for d in (1, 2, 3):
        s0 = s0 + c2in[0, d]
        s1 = s1 + c2in[1, d]
    czout[0] = s0[:8]
    czout[1] = s0[8:]
    czout[2] = s1[:8]
    czout[3] = s1[8:]
    cz = [push("cz", d, czout.at[(z + d) % 4], czin.at[d], at_z(d)) for d in (2, 1, 3)]

    for d in (1, 3, 2):
        eg[d].wait_recv()
        got = egb.at[c, (zh + 4 - d) % 4]
        eh.append(push("eh", d, got, got, other))

    for copy in nc:
        copy.wait_recv()
    rank = proj[...].reshape(512, 128)
    xs = strip[:, :, 0].reshape(512, 768)
    gs = strip[:, :, 1].reshape(512, 768)
    gupout_ref[...] = scaling * tn(rank[:, :64], gs)
    save(0, gupout_ref, gupout_hbm)
    gdin_ref[...] = scaling * tn(rank[:, 64:], xs)
    save(1, gdin_ref, gdin_hbm)

    for copy in eh:
        copy.wait_recv()
    gupin_ref[...] = egb[0].reshape(64, 384).astype(F32)
    gdout_ref[...] = egb[1].reshape(64, 384).astype(F32)
    save(2, gupin_ref, gupin_hbm)
    save(3, gdout_ref, gdout_hbm)

    half = z // 2
    k = (1 - half) * y + half * x
    j = (1 - half) * x + half * y
    rows = proj[half, k, j].astype(F32)
    own = jnp.where(z % 2 == 0, rows[:8], rows[8:])[:, 64:].astype(BF16)
    extra = scaling * nn(own, din_ref[...])
    for copy in cz:
        copy.wait_recv()
    out = czout[z] + extra
    for d in (1, 2, 3):
        out = out + czin[d]
    dx_ref[...] = out.astype(BF16)
    save(4, dx_ref, dx_hbm)

    drain()
    for copy in outs:
        copy.wait()


def hand_over(*refs):
    ins, outs, held, sems = refs[:5], refs[5:10], refs[10:15], refs[15]
    reads = [pltpu.make_async_copy(ins[i], held[i], sems.at[0, i]) for i in range(5)]
    writes = [pltpu.make_async_copy(held[i], outs[i], sems.at[1, i]) for i in range(5)]
    for copy in reads:
        copy.start()
    for read, write in zip(reads, writes):
        read.wait()
        write.start()
    for copy in writes:
        copy.wait()


def shards(x, g, w1, w2, din, upin, dout, upout):
    hbm = pl.BlockSpec(memory_space=pl.ANY)
    nf = len(FAMILIES)
    shapes = (
        jax.ShapeDtypeStruct((8, 768), BF16),
        jax.ShapeDtypeStruct((64, 768), F32),
        jax.ShapeDtypeStruct((64, 384), F32),
        jax.ShapeDtypeStruct((64, 384), F32),
        jax.ShapeDtypeStruct((64, 768), F32),
    )
    made = pl.pallas_call(
        kernel,
        out_shape=shapes,
        in_specs=[hbm] * 8,
        out_specs=(hbm,) * 5,
        scratch_shapes=[
            pltpu.VMEM((8, 768), BF16),
            pltpu.VMEM((8, 768), BF16),
            pltpu.VMEM((768, 384), BF16),
            pltpu.VMEM((384, 768), BF16),
            pltpu.VMEM((64, 768), BF16),
            pltpu.VMEM((64, 384), BF16),
            pltpu.VMEM((64, 384), BF16),
            pltpu.VMEM((64, 768), BF16),
            pltpu.VMEM((4, 16, 768), BF16),
            pltpu.VMEM((2, 4, 2, 4, 16, 768), BF16),
            pltpu.VMEM((4, 2, 4, 16, 768), F32),
            pltpu.VMEM((4, 4, 16, 768), F32),
            pltpu.VMEM((2, 4, 16, 128), F32),
            pltpu.VMEM((4, 16, 128), F32),
            pltpu.VMEM((4, 4, 16, 768), BF16),
            pltpu.VMEM((4, 4, 16, 768), BF16),
            pltpu.VMEM((4, 16, 128), BF16),
            pltpu.VMEM((4, 16, 128), BF16),
            pltpu.VMEM((4, 16, 128), BF16),
            pltpu.VMEM((4, 16, 384), BF16),
            pltpu.VMEM((2, 4, 4, 16, 384), BF16),
            pltpu.VMEM((2, 4, 4, 16, 128), BF16),
            pltpu.VMEM((4, 4, 16, 128), F32),
            pltpu.VMEM((4, 4, 16, 128), F32),
            pltpu.VMEM((4, 4, 16, 128), F32),
            pltpu.VMEM((2, 64, 384), F32),
            pltpu.VMEM((64, 384), F32),
            pltpu.VMEM((4, 16, 384), BF16),
            pltpu.VMEM((4, 16, 384), BF16),
            pltpu.VMEM((2, 4, 16, 384), BF16),
            pltpu.VMEM((2, 4, 4, 16, 768), BF16),
            pltpu.VMEM((2, 4, 4, 16, 768), BF16),
            pltpu.VMEM((2, 4, 16, 768), F32),
            pltpu.VMEM((2, 4, 16, 768), F32),
            pltpu.VMEM((4, 8, 768), F32),
            pltpu.VMEM((4, 8, 768), F32),
        ]
        + [pltpu.VMEM(t.shape, t.dtype) for t in shapes]
        + [
            pltpu.SemaphoreType.DMA((8,)),
            pltpu.SemaphoreType.DMA((5,)),
            pltpu.SemaphoreType.DMA((nf, 4)),
            pltpu.SemaphoreType.DMA((nf, 4)),
        ],
        compiler_params=pltpu.CompilerParams(
            collective_id=0, has_side_effects=True, vmem_limit_bytes=60 * 1024 * 1024
        ),
    )(x, g, w1, w2, din, upin, dout, upout)
    return pl.pallas_call(
        hand_over,
        out_shape=shapes,
        in_specs=[hbm] * 5,
        out_specs=(hbm,) * 5,
        scratch_shapes=[pltpu.VMEM(t.shape, t.dtype) for t in shapes]
        + [pltpu.SemaphoreType.DMA((2, 5))],
        compiler_params=pltpu.CompilerParams(vmem_limit_bytes=60 * 1024 * 1024),
    )(*made)


def solution(mesh):
    return jax.shard_map(
        shards,
        mesh=mesh,
        in_specs=(
            P("wide", "narrow"),
            P("wide", "narrow"),
            P("narrow", "wide"),
            P("wide", "narrow"),
            P(None, "narrow"),
            P(None, "wide"),
            P(None, "wide"),
            P(None, "narrow"),
        ),
        out_specs=(
            P("wide", "narrow"),
            P(None, "narrow"),
            P(None, "wide"),
            P(None, "wide"),
            P(None, "narrow"),
        ),
        check_vma=False,
    )
```

```python
import functools
import math

import jax
import jax.numpy as jnp
from jax import lax
from jax.experimental import pallas as pl
from jax.experimental.pallas import tpu as pltpu
from jax.sharding import PartitionSpec as P

MESH = pl.DeviceIdType.MESH
F32 = jnp.float32
BF16 = jnp.bfloat16
scaling = 2.0
coef = math.sqrt(2.0 / math.pi)

FAMILIES = (
    "gz", "ga", "gb", "gc", "gd", "gf", "gh", "core", "cj", "rz0", "rz1", "rz2", "rz3", "rj", "pj",
    "pz0", "pz1", "pz2", "pz3", "pc0", "pc1", "pc2", "pc3", "fx", "fy", "fz", "nz", "nc",
    "ec", "ez", "eg", "eh", "ya", "xa", "xb", "yb", "cz",
)
FAMILY = {name: i for i, name in enumerate(FAMILIES)}
ORDER = (0, 1, 3, 2)


def nn(left, right):
    return lax.dot_general(left, right, (((1,), (0,)), ((), ())), preferred_element_type=F32)


def nt(left, right):
    return lax.dot_general(left, right, (((1,), (1,)), ((), ())), preferred_element_type=F32)


def tn(left, right):
    return lax.dot_general(left, right, (((0,), (0,)), ((), ())), preferred_element_type=F32)


def kernel(
    x_hbm, g_hbm, w1_hbm, w2_hbm, din_hbm, upin_hbm, dout_hbm, upout_hbm,
    dx_hbm, gdin_hbm, gupin_hbm, gdout_hbm, gupout_hbm,
    x_ref, g_ref, w1, w2, din_ref, upin_ref, dout_ref, upout_ref,
    zbuf, strip, part, part_in, pj, pj_in, red_out, red_in, pj_out, pj_red, pj_all,
    act_all, pre, proj, fxb, fyb, fzb, eown, ein, ezout, ezin, egb,
    dxp, c1in, c2out, c2in, czout, czin,
    dx_ref, gdin_ref, gupin_ref, gdout_ref, gupout_ref, wsem, osem, ssem, rsem,
):
    w = lax.axis_index("wide")
    n = lax.axis_index("narrow")
    y, z, x = w // 16, (w // 4) % 4, w % 4
    zh, c = n // 2, n % 2
    oc = 1 - c

    def at_x(d):
        return (y * 16 + z * 4 + (x + d) % 4, n)

    def at_y(d):
        return (((y + d) % 4) * 16 + z * 4 + x, n)

    def at_z(d):
        return (y * 16 + ((z + d) % 4) * 4 + x, n)

    def at_h(d):
        return (w, ((zh + d) % 4) * 2 + c)

    other = (w, zh * 2 + oc)
    sent = []

    def drain():
        while sent:
            sent.pop(0).wait_send()

    def push(family, slot, src, dst, to):
        i = FAMILY[family]
        copy = pltpu.make_async_remote_copy(
            src_ref=src, dst_ref=dst, send_sem=ssem.at[i, slot], recv_sem=rsem.at[i, slot],
            device_id=to, device_id_type=MESH,
        )
        copy.start()
        sent.append(copy)
        return copy

    outs = []

    def save(i, src, dst):
        copy = pltpu.make_async_copy(src, dst, osem.at[i])
        copy.start()
        outs.append(copy)

    loads = [
        pltpu.make_async_copy(src, dst, wsem.at[i])
        for i, (src, dst) in enumerate((
            (x_hbm, x_ref), (g_hbm, g_ref), (w1_hbm, w1), (w2_hbm, w2), (din_hbm, din_ref),
            (upin_hbm, upin_ref), (dout_hbm, dout_ref), (upout_hbm, upout_ref),
        ))
    ]
    for load in loads:
        load.start()

    barrier = pltpu.get_barrier_semaphore()
    for d in (1, 2, 3):
        for at in (at_x, at_y, at_z, at_h):
            pl.semaphore_signal(barrier, inc=1, device_id=at(d), device_id_type=MESH)
    pl.semaphore_signal(barrier, inc=1, device_id=other, device_id_type=MESH)

    loads[0].wait()
    loads[1].wait()
    zbuf[z] = jnp.concatenate([x_ref[...].astype(F32), g_ref[...].astype(F32)], 0).astype(BF16)
    pl.semaphore_wait(barrier, 13)

    copies = [push("gz", d, zbuf.at[z], zbuf.at[z], at_z(d)) for d in (2, 1, 3)]
    for copy in copies:
        copy.wait_recv()
    planes = [zbuf[i].astype(F32) for i in range(4)]
    for t in range(2):
        rows = slice(8 * t, 8 * t + 8)
        strip[0, y, t, x] = jnp.concatenate([planes[0][rows], planes[1][rows]], 0).astype(BF16)
        strip[1, x, t, y] = jnp.concatenate([planes[2][rows], planes[3][rows]], 0).astype(BF16)
    copies = []
    for d in (2, 1, 3):
        mine = strip.at[0, y, :, x]
        copies.append(push("ga", d, mine, mine, at_x(d)))
        mine = strip.at[1, x, :, y]
        copies.append(push("gb", d, mine, mine, at_y(d)))
    for copy in copies:
        copy.wait_recv()
    gc, gd = {}, {}
    for d in (1, 3):
        mine = strip.at[0, y]
        gc[d] = push("gc", d, mine, mine, at_y(d))
        mine = strip.at[1, x]
        gd[d] = push("gd", d, mine, mine, at_x(d))
    for load in loads[2:]:
        load.wait()

    core = {}

    def multiply(d):
        ka, kb = (y + 4 - d) % 4, (x + 4 - d) % 4
        xs = jnp.concatenate([strip[0, ka, 0].reshape(64, 768), strip[1, kb, 0].reshape(64, 768)], 0)
        gs = jnp.concatenate([strip[0, ka, 1].reshape(64, 768), strip[1, kb, 1].reshape(64, 768)], 0)
        hp = nn(xs, w1[...])
        bp = nt(gs, w2[...])
        for h in range(2):
            rows = slice(64 * h, 64 * h + 64)
            part[d, h, :, :, :384] = hp[rows].reshape(4, 16, 384)
            part[d, h, :, :, 384:] = bp[rows].reshape(4, 16, 384)
        core[d] = push("core", d, part.at[d, oc], part_in.at[d], other)
        if d == 0:
            both = jnp.concatenate([nt(xs, din_ref[...]), nt(gs, upout_ref[...])], 1)
            pj[...] = both.reshape(2, 4, 16, 128)
            core["j"] = push("cj", 0, pj.at[oc], pj_in, other)

    rz = {}

    def scatter(d):
        core[d].wait_recv()
        red_out[d] = (part[d, c] + part_in[d]).astype(BF16)
        rz[d] = [
            push("rz%d" % d, e, red_out.at[d, (zh + e) % 4], red_in.at[e, d], at_h(e))
            for e in (2, 1, 3)
        ]
        if d == 0:
            core["j"].wait_recv()
            pj_out[...] = (pj[c] + pj_in[...]).astype(BF16)
            rz["j"] = [
                push("rj", e, pj_out.at[(zh + e) % 4], pj_red.at[e], at_h(e)) for e in (2, 1, 3)
            ]

    multiply(0)
    scatter(0)
    far = []
    for t, d in ((0, 1), (1, 3)):
        gc[d].wait_recv()
        got = strip.at[0, (y + 4 - d) % 4, t]
        far.append(push("gf", d, got, got, at_y(d)))
        gd[d].wait_recv()
        got = strip.at[1, (x + 4 - d) % 4, t]
        far.append(push("gh", d, got, got, at_x(d)))
    multiply(1)
    multiply(3)
    scatter(1)
    scatter(3)
    for copy in far:
        copy.wait_recv()
    multiply(2)
    for copy in rz["j"]:
        copy.wait_recv()
    total = pj[c, zh] + pj_in[zh]
    for e in (1, 2, 3):
        total = total + pj_red[e].astype(F32)
    pj_all[0] = total.astype(BF16)
    pjc = {}
    for d in (2, 1, 3):
        to = (oc * at_y(d)[0] + c * at_x(d)[0], n)
        pjc[d] = push("pj", d, pj_all.at[0], pj_all.at[d], to)
    scatter(2)

    pz, pc = {}, {}

    def activate(d):
        for copy in rz[d]:
            copy.wait_recv()
        if d:
            pjc[d].wait_recv()
        total = part[d, c, zh] + part_in[d, zh]
        for e in (1, 2, 3):
            total = total + red_in[e, d].astype(F32)
        both = pj_all[d]
        v = total[:, :384] + scaling * nn(both[:, :64], upin_ref[...])
        grad = total[:, 384:] + scaling * nn(both[:, 64:], dout_ref[...])
        t = jnp.tanh(coef * (v + 0.044715 * v * v * v))
        act_all[d] = (0.5 * v * (1.0 + t)).astype(BF16)
        slope = 0.5 * (1.0 + t) + 0.5 * v * (1.0 - t * t) * coef * (1.0 + 3.0 * 0.044715 * v * v)
        pre[c, zh, d] = (grad * slope).astype(BF16)
        mine = pre.at[c, zh, d]
        pz[d] = {e: push("pz%d" % d, e, mine, mine, at_h(e)) for e in (2, 1, 3)}
        pc[d] = [push("pc%d" % d, 0, mine, mine, other)]

    def forward(d):
        for e in (1, 3, 2):
            pz[d][e].wait_recv()
            got = pre.at[c, (zh + 4 - e) % 4, d]
            pc[d].append(push("pc%d" % d, e, got, got, other))

    c1 = []

    def back(d):
        for copy in pc[d]:
            copy.wait_recv()
        rows = jnp.concatenate([pre[0, :, d].reshape(64, 384), pre[1, :, d].reshape(64, 384)], 0)
        value = nt(rows, w1[...]).astype(BF16)
        dxp[0, d] = value[:64].reshape(4, 16, 768)
        dxp[1, d] = value[64:].reshape(4, 16, 768)
        if d:
            e = 4 - d
            c1.append(push("ya", e, dxp.at[0, d], c1in.at[0, e], at_y(e)))
            c1.append(push("xb", e, dxp.at[1, d], c1in.at[1, e], at_x(e)))

    for d in ORDER:
        activate(d)

    acts = act_all[...].reshape(64, 384)
    pres = pre[c, zh].reshape(64, 384)
    both = jnp.concatenate([nt(acts, dout_ref[...]), nt(pres, upin_ref[...])], 1).reshape(4, 16, 128)
    for d in range(4):
        fxb[x, oc * ((y + 4 - d) % 4) + c * ((x + 4 - d) % 4)] = both[d]
    fx = [push("fx", d, fxb.at[x], fxb.at[x], at_x(d)) for d in (2, 1, 3)]
    ranks = pj_all[...].reshape(64, 128)
    eown[0] = scaling * tn(ranks[:, :64], pres)
    eown[1] = scaling * tn(ranks[:, 64:], acts)
    ec = push("ec", 0, eown.at[oc], ein, other)
    forward(0)
    for copy in fx:
        copy.wait_recv()
    fyb[y] = fxb[0] + fxb[1] + fxb[2] + fxb[3]
    fy = [push("fy", d, fyb.at[y], fyb.at[y], at_y(d)) for d in (2, 1, 3)]
    forward(1)
    back(0)
    ec.wait_recv()
    ezout[...] = (eown[c] + ein[...]).astype(BF16).reshape(4, 16, 384)
    ez = [push("ez", d, ezout.at[(zh + d) % 4], ezin.at[d], at_h(d)) for d in (2, 1, 3)]
    for copy in fy:
        copy.wait_recv()
    fzb[z] = (fyb[0] + fyb[1] + fyb[2] + fyb[3]).astype(BF16)
    fz = [push("fz", d, fzb.at[z], fzb.at[z], at_z(d)) for d in (2, 1, 3)]
    forward(3)
    back(1)
    drain()
    forward(2)
    back(3)
    back(2)

    for copy in fz:
        copy.wait_recv()
    proj[c, :, zh] = sum(fzb[i].astype(F32) for i in range(4)).astype(BF16)
    mine = proj.at[c, :, zh]
    nz = {d: push("nz", d, mine, mine, at_h(d)) for d in (2, 1, 3)}
    nc = [push("nc", 0, mine, mine, other)]

    for copy in ez:
        copy.wait_recv()
    esl = ezout[zh].astype(F32)
    for d in (1, 2, 3):
        esl = esl + ezin[d].astype(F32)
    egb[c, zh] = esl.astype(BF16)
    mine = egb.at[c, zh]
    eg = {d: push("eg", d, mine, mine, at_h(d)) for d in (2, 1, 3)}
    eh = [push("eh", 0, mine, mine, other)]

    for copy in c1:
        copy.wait_recv()
    c2 = []
    s0 = dxp[0, 0].astype(F32)
    s1 = dxp[1, 0].astype(F32)
    for d in (1, 2, 3):
        s0 = s0 + c1in[0, d].astype(F32)
        s1 = s1 + c1in[1, d].astype(F32)
    c2out[0] = s0.astype(BF16)
    c2out[1] = s1.astype(BF16)
    for d in (2, 1, 3):
        c2.append(push("xa", d, c2out.at[0, (x + d) % 4], c2in.at[0, d], at_x(d)))
        c2.append(push("yb", d, c2out.at[1, (y + d) % 4], c2in.at[1, d], at_y(d)))

    for d in (1, 3, 2):
        nz[d].wait_recv()
        got = proj.at[c, :, (zh + 4 - d) % 4]
        nc.append(push("nc", d, got, got, other))

    for copy in c2:
        copy.wait_recv()
    s0 = c2out[0, x].astype(F32)
    s1 = c2out[1, y].astype(F32)
    for d in (1, 2, 3):
        s0 = s0 + c2in[0, d].astype(F32)
        s1 = s1 + c2in[1, d].astype(F32)
    czout[0] = s0[:8]
    czout[1] = s0[8:]
    czout[2] = s1[:8]
    czout[3] = s1[8:]
    cz = [push("cz", d, czout.at[(z + d) % 4], czin.at[d], at_z(d)) for d in (2, 1, 3)]

    for d in (1, 3, 2):
        eg[d].wait_recv()
        got = egb.at[c, (zh + 4 - d) % 4]
        eh.append(push("eh", d, got, got, other))

    for copy in nc:
        copy.wait_recv()
    rank = proj[...].reshape(512, 128)
    xs = strip[:, :, 0].reshape(512, 768)
    gs = strip[:, :, 1].reshape(512, 768)
    gupout_ref[...] = scaling * tn(rank[:, :64], gs)
    save(0, gupout_ref, gupout_hbm)
    gdin_ref[...] = scaling * tn(rank[:, 64:], xs)
    save(1, gdin_ref, gdin_hbm)

    for copy in eh:
        copy.wait_recv()
    gupin_ref[...] = egb[0].reshape(64, 384).astype(F32)
    gdout_ref[...] = egb[1].reshape(64, 384).astype(F32)
    save(2, gupin_ref, gupin_hbm)
    save(3, gdout_ref, gdout_hbm)

    half = z // 2
    k = (1 - half) * y + half * x
    j = (1 - half) * x + half * y
    rows = proj[half, k, j].astype(F32)
    own = jnp.where(z % 2 == 0, rows[:8], rows[8:])[:, 64:].astype(BF16)
    extra = scaling * nn(own, din_ref[...])
    for copy in cz:
        copy.wait_recv()
    out = czout[z] + extra
    for d in (1, 2, 3):
        out = out + czin[d]
    dx_ref[...] = out.astype(BF16)
    save(4, dx_ref, dx_hbm)

    drain()
    for copy in outs:
        copy.wait()


def hand_over(*refs):
    ins, outs, held, sems = refs[:5], refs[5:10], refs[10:15], refs[15]
    reads = [pltpu.make_async_copy(ins[i], held[i], sems.at[0, i]) for i in range(5)]
    writes = [pltpu.make_async_copy(held[i], outs[i], sems.at[1, i]) for i in range(5)]
    for copy in reads:
        copy.start()
    for read, write in zip(reads, writes):
        read.wait()
        write.start()
    for copy in writes:
        copy.wait()


def shards(x, g, w1, w2, din, upin, dout, upout):
    hbm = pl.BlockSpec(memory_space=pl.ANY)
    nf = len(FAMILIES)
    shapes = (
        jax.ShapeDtypeStruct((8, 768), BF16),
        jax.ShapeDtypeStruct((64, 768), F32),
        jax.ShapeDtypeStruct((64, 384), F32),
        jax.ShapeDtypeStruct((64, 384), F32),
        jax.ShapeDtypeStruct((64, 768), F32),
    )
    made = pl.pallas_call(
        kernel,
        out_shape=shapes,
        in_specs=[hbm] * 8,
        out_specs=(hbm,) * 5,
        scratch_shapes=[
            pltpu.VMEM((8, 768), BF16),
            pltpu.VMEM((8, 768), BF16),
            pltpu.VMEM((768, 384), BF16),
            pltpu.VMEM((384, 768), BF16),
            pltpu.VMEM((64, 768), BF16),
            pltpu.VMEM((64, 384), BF16),
            pltpu.VMEM((64, 384), BF16),
            pltpu.VMEM((64, 768), BF16),
            pltpu.VMEM((4, 16, 768), BF16),
            pltpu.VMEM((2, 4, 2, 4, 16, 768), BF16),
            pltpu.VMEM((4, 2, 4, 16, 768), F32),
            pltpu.VMEM((4, 4, 16, 768), F32),
            pltpu.VMEM((2, 4, 16, 128), F32),
            pltpu.VMEM((4, 16, 128), F32),
            pltpu.VMEM((4, 4, 16, 768), BF16),
            pltpu.VMEM((4, 4, 16, 768), BF16),
            pltpu.VMEM((4, 16, 128), BF16),
            pltpu.VMEM((4, 16, 128), BF16),
            pltpu.VMEM((4, 16, 128), BF16),
            pltpu.VMEM((4, 16, 384), BF16),
            pltpu.VMEM((2, 4, 4, 16, 384), BF16),
            pltpu.VMEM((2, 4, 4, 16, 128), BF16),
            pltpu.VMEM((4, 4, 16, 128), F32),
            pltpu.VMEM((4, 4, 16, 128), F32),
            pltpu.VMEM((4, 4, 16, 128), BF16),
            pltpu.VMEM((2, 64, 384), F32),
            pltpu.VMEM((64, 384), F32),
            pltpu.VMEM((4, 16, 384), BF16),
            pltpu.VMEM((4, 16, 384), BF16),
            pltpu.VMEM((2, 4, 16, 384), BF16),
            pltpu.VMEM((2, 4, 4, 16, 768), BF16),
            pltpu.VMEM((2, 4, 4, 16, 768), BF16),
            pltpu.VMEM((2, 4, 16, 768), BF16),
            pltpu.VMEM((2, 4, 16, 768), BF16),
            pltpu.VMEM((4, 8, 768), F32),
            pltpu.VMEM((4, 8, 768), F32),
        ]
        + [pltpu.VMEM(t.shape, t.dtype) for t in shapes]
        + [
            pltpu.SemaphoreType.DMA((8,)),
            pltpu.SemaphoreType.DMA((5,)),
            pltpu.SemaphoreType.DMA((nf, 4)),
            pltpu.SemaphoreType.DMA((nf, 4)),
        ],
        compiler_params=pltpu.CompilerParams(
            collective_id=0, has_side_effects=True, vmem_limit_bytes=60 * 1024 * 1024
        ),
    )(x, g, w1, w2, din, upin, dout, upout)
    return pl.pallas_call(
        hand_over,
        out_shape=shapes,
        in_specs=[hbm] * 5,
        out_specs=(hbm,) * 5,
        scratch_shapes=[pltpu.VMEM(t.shape, t.dtype) for t in shapes]
        + [pltpu.SemaphoreType.DMA((2, 5))],
        compiler_params=pltpu.CompilerParams(vmem_limit_bytes=60 * 1024 * 1024),
    )(*made)


def solution(mesh):
    return jax.shard_map(
        shards,
        mesh=mesh,
        in_specs=(
            P("wide", "narrow"),
            P("wide", "narrow"),
            P("narrow", "wide"),
            P("wide", "narrow"),
            P(None, "narrow"),
            P(None, "wide"),
            P(None, "wide"),
            P(None, "narrow"),
        ),
        out_specs=(
            P("wide", "narrow"),
            P(None, "narrow"),
            P(None, "wide"),
            P(None, "wide"),
            P(None, "narrow"),
        ),
        check_vma=False,
    )
```
